32 devices in a mesh: crops: 2 (over y), row: 4 (over z), sub: 2 (over x), pair: 2 (over core).
Axes of the slice: x: 2, y: 2, z: 4, core: 2. Of those that a mesh axis runs over, the one named last changes fastest.
Arguments:
- pair_act: bfloat16 [64, 32, 128], P(('crops', 'row'), ('sub', 'pair')), parts along dimension 0, may hold values from -6 to 6
- residue_mask: int32 [64], P('crops'), parts along dimension 0, may hold values 0 or 1
- w_proj: bfloat16 [128, 512], replicated, may hold values from -0.5 to 0.5
- w_gate: bfloat16 [128, 128], replicated, may hold values from -0.5 to 0.5
- w_out: bfloat16 [128, 128], replicated, may hold values from -0.5 to 0.5
- d_transposed: bfloat16 [64, 32, 128], P(('crops', 'row', 'sub', 'pair')), parts along dimension 0, may hold values from -6 to 6
Outputs:
- transposed: bfloat16 [64, 32, 128], P(('crops', 'row', 'sub', 'pair')), parts along dimension 0
- d_pair: bfloat16 [64, 32, 128], P(('crops', 'row'), ('sub', 'pair')), parts along dimension 0
- g_proj: float32 [256, 512], P('crops'), parts along dimension 0
- g_gate: float32 [256, 128], P('crops'), parts along dimension 0
- g_out: float32 [256, 128], P('crops'), parts along dimension 0
The draws below stay inside these ranges and needn't reach their ends.
There are 2 independent parts, one for each index of `crops`. The reference program is written for one: setup_inputs(seed, part) draws one part's arguments, and reference() takes and returns one part's arrays. A program takes and returns all parts, laid end to end along the dimension named above; an argument that names none is the same for every part. Nothing has to cross between parts.
All inputs are finite; a program needn't handle non-finite values.
Results may differ from the reference program's by a relative error of at most 0.0088.
Values may be sent and summed in bfloat16 or wider, within the bound.
A program may use at most 64 MiB of HBM per device.

```python
import jax
import jax.numpy as jnp
from jax import lax

C = 128
CH = 128
N = 32


def plant(entries, stream_key, low, high):
    shape = entries.shape
    index_at = [jax.random.randint(jax.random.fold_in(stream_key, axis), (), 0, shape[axis]) for axis in range(len(shape))]
    entries = entries.at[tuple(index_at)].set(low)
    longest = shape.index(max(shape))
    index_at[longest] = (index_at[longest] + 1) % shape[longest]
    return entries.at[tuple(index_at)].set(high)


def levels(stream_key, extent, split, least, top_value):
    loudness, own = 1.0, jax.random.fold_in(stream_key, 6)
    for axis_at, shards_of in split:
        steps = jnp.exp(jax.random.uniform(jax.random.fold_in(own, axis_at), (shards_of,), jnp.float32, least / len(split), top_value / len(split)))
        loudness = loudness * jnp.repeat(steps, extent[axis_at] // shards_of).reshape([-1 if axis == axis_at else 1 for axis in range(len(extent))])
    return loudness


def bell_draw(rng, shape, width, most, cuts=(), held_as=jnp.bfloat16):
    result = width * jax.random.normal(rng, shape, jnp.float32)
    if cuts:
        result = result * levels(rng, shape, cuts, -0.22, 0.18)
    return jnp.clip(result, -most, most).astype(held_as)


def setup_inputs(seed: int = 0, part: int = 0) -> dict:
    keys = jax.random.split(jax.random.key(seed), 7)
    own_keys = jax.random.split(jax.random.fold_in(keys[6], part), 7)
    return {
        "pair_act": bell_draw(own_keys[0], (N, N, C), 1.0, 6.0, ((0, 4), (1, 4))),
        "residue_mask": plant((jax.random.randint(own_keys[1], (N,), 0, 4) < 3).astype(jnp.int32), jax.random.fold_in(own_keys[1], 1), 0, 1),
        "w_proj": bell_draw(keys[2], (C, 4 * CH), C ** -0.5, 0.5),
        "w_gate": bell_draw(keys[3], (C, C), C ** -0.5, 0.5),
        "w_out": bell_draw(keys[4], (CH, C), CH ** -0.5, 0.5),
        "d_transposed": bell_draw(own_keys[5], (N, N, C), 1.0, 6.0, ((0, 16),)),
    }


epsilon = 1e-05

def layer_norm(values):
    row_mean = lax.optimization_barrier(jnp.mean(values, axis=-1, keepdims=True))
    centred = values - row_mean
    row_var = lax.optimization_barrier(jnp.mean(centred * centred, axis=-1, keepdims=True))
    return centred * lax.rsqrt(row_var + epsilon)

def norm_back(values, cotangent):
    return jax.vjp(layer_norm, values)[1](cotangent)[0]

def front_forward(pair_rows, w_proj, w_gate, pair_mask):
    hidden_width = w_proj.shape[1] // 4
    normed = layer_norm(pair_rows).astype(jnp.bfloat16)
    projected = jnp.dot(normed, w_proj, preferred_element_type=jnp.float32)
    gate_pre = jnp.dot(normed, w_gate, preferred_element_type=jnp.float32)
    left_b = jax.nn.sigmoid(projected[:, :hidden_width]) * projected[:, hidden_width:2 * hidden_width] * pair_mask
    right_b = jax.nn.sigmoid(projected[:, 2 * hidden_width:3 * hidden_width]) * projected[:, 3 * hidden_width:] * pair_mask
    return (normed, projected, left_b.astype(jnp.bfloat16), right_b.astype(jnp.bfloat16), jax.nn.sigmoid(gate_pre))

def back_forward(crossed_rows, gate_act, pair_rows, w_out):
    normed_x = layer_norm(crossed_rows.astype(jnp.float32)).astype(jnp.bfloat16)
    out_proj = jnp.dot(normed_x, w_out, preferred_element_type=jnp.float32)
    return (normed_x, out_proj, pair_rows + gate_act * out_proj)

def back_backward(crossed_rows, out_proj, gate_act, w_out, d_up):
    d_out_b = (gate_act * d_up).astype(jnp.bfloat16)
    d_gate_b = (out_proj * d_up * gate_act * (1.0 - gate_act)).astype(jnp.bfloat16)
    d_normed_x = jnp.dot(d_out_b, w_out.T, preferred_element_type=jnp.float32)
    d_cross_b = norm_back(crossed_rows.astype(jnp.float32), d_normed_x).astype(jnp.bfloat16)
    return (d_out_b, d_gate_b, d_cross_b)

def front_backward(pair_rows, projected, pair_mask, d_left, d_right, d_gate_b, w_proj, w_gate, d_up):
    hidden_width = w_proj.shape[1] // 4
    left_gate = jax.nn.sigmoid(projected[:, :hidden_width])
    left_value = projected[:, hidden_width:2 * hidden_width]
    right_gate = jax.nn.sigmoid(projected[:, 2 * hidden_width:3 * hidden_width])
    right_value = projected[:, 3 * hidden_width:]
    d_proj = jnp.concatenate([d_left * left_value * pair_mask * left_gate * (1.0 - left_gate), d_left * left_gate * pair_mask, d_right * right_value * pair_mask * right_gate * (1.0 - right_gate), d_right * right_gate * pair_mask], axis=1).astype(jnp.bfloat16)
    d_normed = jnp.dot(d_proj, w_proj.T, preferred_element_type=jnp.float32) + jnp.dot(d_gate_b, w_gate.T, preferred_element_type=jnp.float32)
    d_pair = (d_up + norm_back(pair_rows, d_normed)).astype(jnp.bfloat16)
    return (d_proj, d_pair)

def reference(pair_act, residue_mask, w_proj, w_gate, w_out, d_transposed):
    highest = lax.Precision.HIGHEST
    residue_valid = residue_mask.astype(jnp.float32)
    pair_mask = (residue_valid[:, None] * residue_valid[None, :]).reshape(N * N, 1)
    pair_rows = pair_act.reshape(N * N, C).astype(jnp.float32)
    normed, projected, left_b, right_b, gate_act = front_forward(pair_rows, w_proj, w_gate, pair_mask)
    left_t = left_b.reshape(N, N, CH).transpose(2, 0, 1).astype(jnp.float32)
    right_t = right_b.reshape(N, N, CH).transpose(2, 0, 1).astype(jnp.float32)
    crossed = jnp.einsum('cik,cjk->cij', left_t, right_t, precision=highest)
    crossed_rows = crossed.astype(jnp.bfloat16).transpose(1, 2, 0).reshape(N * N, CH)
    normed_x, out_proj, updated = back_forward(crossed_rows, gate_act, pair_rows, w_out)
    transposed = updated.astype(jnp.bfloat16).reshape(N, N, C).transpose(1, 0, 2)
    d_up = d_transposed.transpose(1, 0, 2).reshape(N * N, C).astype(jnp.float32)
    d_out_b, d_gate_b, d_cross_b = back_backward(crossed_rows, out_proj, gate_act, w_out, d_up)
    d_cross = d_cross_b.reshape(N, N, CH).transpose(2, 0, 1).astype(jnp.float32)
    d_left = jnp.einsum('cij,cjk->cik', d_cross, right_t, precision=highest)
    d_right = jnp.einsum('cij,cik->cjk', d_cross, left_t, precision=highest)
    d_left_rows = d_left.astype(jnp.bfloat16).transpose(1, 2, 0).reshape(N * N, CH).astype(jnp.float32)
    d_right_rows = d_right.astype(jnp.bfloat16).transpose(1, 2, 0).reshape(N * N, CH).astype(jnp.float32)
    d_proj, d_pair = front_backward(pair_rows, projected, pair_mask, d_left_rows, d_right_rows, d_gate_b, w_proj, w_gate, d_up)
    g_proj = jnp.dot(normed.T, d_proj, preferred_element_type=jnp.float32) / N
    g_gate = jnp.dot(normed.T, d_gate_b, preferred_element_type=jnp.float32) / N
    g_out = jnp.dot(normed_x.T, d_out_b, preferred_element_type=jnp.float32) / N
    return (transposed, d_pair.reshape(N, N, C), g_proj, g_gate, g_out)
```

```python
import functools

import jax
import jax.numpy as jnp
from jax import lax
from jax.experimental import pallas as pl
from jax.experimental.pallas import tpu as pltpu
from jax.sharding import PartitionSpec as P

epsilon = 1e-05


def layer_norm(values):
    row_mean = jnp.mean(values, axis=-1, keepdims=True)
    centred = values - row_mean
    row_var = jnp.mean(centred * centred, axis=-1, keepdims=True)
    return centred * lax.rsqrt(row_var + epsilon)


def norm_back(values, cotangent):
    return jax.vjp(layer_norm, values)[1](cotangent)[0]


def front_forward(pair_rows, w_proj, w_gate, pair_mask):
    hidden_width = w_proj.shape[1] // 4
    normed = layer_norm(pair_rows).astype(jnp.bfloat16)
    projected = jnp.dot(normed, w_proj, preferred_element_type=jnp.float32)
    gate_pre = jnp.dot(normed, w_gate, preferred_element_type=jnp.float32)
    left_b = (
        jax.nn.sigmoid(projected[:, :hidden_width])
        * projected[:, hidden_width : 2 * hidden_width]
        * pair_mask
    )
    right_b = (
        jax.nn.sigmoid(projected[:, 2 * hidden_width : 3 * hidden_width])
        * projected[:, 3 * hidden_width :]
        * pair_mask
    )
    return (
        normed,
        projected,
        left_b.astype(jnp.bfloat16),
        right_b.astype(jnp.bfloat16),
        jax.nn.sigmoid(gate_pre),
    )


def back_forward(crossed_rows, gate_act, pair_rows, w_out):
    normed_x = layer_norm(crossed_rows.astype(jnp.float32)).astype(jnp.bfloat16)
    out_proj = jnp.dot(normed_x, w_out, preferred_element_type=jnp.float32)
    return (normed_x, out_proj, pair_rows + gate_act * out_proj)


def back_backward(crossed_rows, out_proj, gate_act, w_out, d_up):
    d_out_b = (gate_act * d_up).astype(jnp.bfloat16)
    d_gate_b = (out_proj * d_up * gate_act * (1.0 - gate_act)).astype(jnp.bfloat16)
    d_normed_x = jnp.dot(d_out_b, w_out.T, preferred_element_type=jnp.float32)
    d_cross_b = norm_back(crossed_rows.astype(jnp.float32), d_normed_x).astype(jnp.bfloat16)
    return (d_out_b, d_gate_b, d_cross_b)


def front_backward(
    pair_rows, projected, pair_mask, d_left, d_right, d_gate_b, w_proj, w_gate, d_up
):
    hidden_width = w_proj.shape[1] // 4
    left_gate = jax.nn.sigmoid(projected[:, :hidden_width])
    left_value = projected[:, hidden_width : 2 * hidden_width]
    right_gate = jax.nn.sigmoid(projected[:, 2 * hidden_width : 3 * hidden_width])
    right_value = projected[:, 3 * hidden_width :]
    d_proj = jnp.concatenate(
        [
            d_left * left_value * pair_mask * left_gate * (1.0 - left_gate),
            d_left * left_gate * pair_mask,
            d_right * right_value * pair_mask * right_gate * (1.0 - right_gate),
            d_right * right_gate * pair_mask,
        ],
        axis=1,
    ).astype(jnp.bfloat16)
    d_normed = jnp.dot(d_proj, w_proj.T, preferred_element_type=jnp.float32) + jnp.dot(
        d_gate_b, w_gate.T, preferred_element_type=jnp.float32
    )
    d_pair = (d_up + norm_back(pair_rows, d_normed)).astype(jnp.bfloat16)
    return (d_proj, d_pair)


def to_channels(stacked, row_block, col_block):
    groups = stacked.shape[0]
    col_groups = lax.axis_size(("sub", "pair"))
    sectioning = stacked[None]
    arrived = lax.all_to_all(sectioning, ("sub", "pair"), split_axis=2, concat_axis=0, tiled=True)
    channel_share = arrived.shape[2]
    arrived = arrived.reshape(col_groups, groups, channel_share, row_block, col_block)
    return arrived.transpose(1, 2, 3, 0, 4).reshape(
        groups, channel_share, row_block, col_groups * col_block
    )


def from_channels(stacked, row_block, col_block):
    groups = stacked.shape[0]
    arrived = lax.all_to_all(stacked, ("sub", "pair"), split_axis=3, concat_axis=1, tiled=True)
    return arrived.transpose(0, 2, 3, 1).reshape(groups, row_block * col_block, arrived.shape[1])


def on_device(pair_act, residue_mask, w_proj, w_gate, w_out, d_transposed):
    row_block, col_block, channels = pair_act.shape
    row_count = lax.axis_size("row")
    col_groups = lax.axis_size(("sub", "pair"))
    crop_length = row_block * row_count
    block_width = col_block // row_count
    group_width = row_count // col_groups
    local_rows = row_block * col_block
    row_start = lax.axis_index("row") * row_block
    col_start = lax.axis_index(("sub", "pair")) * col_block
    row_valid = lax.dynamic_slice_in_dim(residue_mask, row_start, row_block, 0).astype(jnp.float32)
    col_valid = lax.dynamic_slice_in_dim(residue_mask, col_start, col_block, 0).astype(jnp.float32)
    pair_mask = (row_valid[:, None] * col_valid[None, :]).reshape(local_rows, 1)
    pair_rows = pair_act.reshape(local_rows, channels).astype(jnp.float32)
    normed, projected, left_b, right_b, gate_act = front_forward(
        pair_rows, w_proj, w_gate, pair_mask
    )
    paired = to_channels(jnp.stack([left_b.T, right_b.T]), row_block, col_block)
    left_t = paired[0]
    right_t = paired[1]
    crossed = jnp.einsum(
        "cik,cjk->cij",
        left_t,
        lax.all_gather(right_t, "row", axis=1, tiled=True),
        preferred_element_type=jnp.float32,
    )
    crossed_rows = from_channels(crossed.astype(jnp.bfloat16)[None], row_block, col_block)[0]
    normed_x, out_proj, updated = back_forward(crossed_rows, gate_act, pair_rows, w_out)
    updated_b = updated.astype(jnp.bfloat16).reshape(
        row_block, group_width, col_groups, block_width, channels
    )
    spread_cols = lax.all_to_all(
        updated_b, ("sub", "pair"), split_axis=2, concat_axis=2, tiled=True
    )
    regrouped = spread_cols.transpose(2, 1, 0, 3, 4).reshape(
        row_count, row_block, block_width, channels
    )
    turned = lax.all_to_all(regrouped, "row", split_axis=0, concat_axis=1, tiled=True)
    transposed = turned.reshape(crop_length, block_width, channels).transpose(1, 0, 2)
    back_in = d_transposed.transpose(1, 0, 2).reshape(row_count, row_block, block_width, channels)
    returned = lax.all_to_all(back_in, "row", split_axis=0, concat_axis=0, tiled=True)
    regrouped_back = returned.reshape(
        col_groups, group_width, row_block, block_width, channels
    ).transpose(2, 1, 0, 3, 4)
    restored = lax.all_to_all(
        regrouped_back, ("sub", "pair"), split_axis=2, concat_axis=2, tiled=True
    )
    d_up = restored.reshape(local_rows, channels).astype(jnp.float32)
    d_out_b, d_gate_b, d_cross_b = back_backward(crossed_rows, out_proj, gate_act, w_out, d_up)
    d_cross_t = to_channels(d_cross_b.T[None], row_block, col_block)[0]
    d_cross_cols = lax.all_to_all(d_cross_t, "row", split_axis=2, concat_axis=1, tiled=True)
    left_part = jnp.einsum(
        "cij,cjk->cik",
        d_cross_t,
        lax.all_gather(right_t, "row", axis=1, tiled=True),
        preferred_element_type=jnp.float32,
    )
    right_part = jnp.einsum(
        "cij,cik->cjk",
        d_cross_cols,
        lax.all_gather(left_t, "row", axis=1, tiled=True),
        preferred_element_type=jnp.float32,
    )
    d_rows_back = from_channels(
        jnp.stack([left_part, right_part]).astype(jnp.bfloat16), row_block, col_block
    )
    d_proj, d_pair = front_backward(
        pair_rows,
        projected,
        pair_mask,
        d_rows_back[0].astype(jnp.float32),
        d_rows_back[1].astype(jnp.float32),
        d_gate_b,
        w_proj,
        w_gate,
        d_up,
    )
    weight_terms = (
        jnp.einsum("rc,rd->cd", normed, d_proj, preferred_element_type=jnp.float32),
        jnp.einsum("rc,rd->cd", normed, d_gate_b, preferred_element_type=jnp.float32),
        jnp.einsum("rc,rd->cd", normed_x, d_out_b, preferred_element_type=jnp.float32),
    )
    g_proj, g_gate, g_out = lax.psum(
        (weight_terms[0], weight_terms[1], weight_terms[2]), ("row", "sub", "pair")
    )
    return (
        transposed,
        d_pair.reshape(row_block, col_block, channels),
        g_proj / crop_length,
        g_gate / crop_length,
        g_out / crop_length,
    )


MESH = pl.DeviceIdType.MESH
F32 = jnp.float32
BF16 = jnp.bfloat16


def gather_kernel(sizes, pair_ref, cot_ref, all_ref, send_sem, recv_sem):
    rows, subs, pairs = sizes
    r, x, c = lax.axis_index("row"), lax.axis_index("sub"), lax.axis_index("pair")
    half = pair_ref.shape[0]

    def slot(row, sub, pair):
        return (row * subs + sub) * pairs + pair

    def copy(owner, number, **target):
        return pltpu.make_async_remote_copy(
            src_ref=all_ref.at[owner],
            dst_ref=all_ref.at[owner],
            send_sem=send_sem.at[number],
            recv_sem=recv_sem.at[owner],
            device_id=target,
            device_id_type=MESH,
        )

    me = slot(r, x, c)
    all_ref[me, :half] = pair_ref[...]
    all_ref[me, half:] = cot_ref[...]

    row_peers = [lax.rem(r + step, rows) for step in range(1, rows)]
    barrier = pltpu.get_barrier_semaphore()
    for peer in row_peers:
        pl.semaphore_signal(barrier, inc=1, device_id={"row": peer}, device_id_type=MESH)
    pl.semaphore_signal(barrier, inc=1, device_id={"sub": 1 - x}, device_id_type=MESH)
    pl.semaphore_signal(barrier, inc=1, device_id={"pair": 1 - c}, device_id_type=MESH)
    pl.semaphore_wait(barrier, rows + 1)

    sent = []

    def send(owner, **target):
        one = copy(owner, len(sent), **target)
        one.start()
        sent.append(one)

    for peer in row_peers:
        send(me, row=peer)
    send(me, sub=1 - x)
    send(me, pair=1 - c)
    for peer in row_peers:
        owner = slot(peer, x, c)
        copy(owner, 0, row=peer).wait_recv()
        send(owner, sub=1 - x)
        send(owner, pair=1 - c)
    for peer in [r] + row_peers:
        owner = slot(peer, 1 - x, c)
        copy(owner, 0, sub=1 - x).wait_recv()
        send(owner, pair=1 - c)
    for peer in [r] + row_peers:
        for sub in (x, 1 - x):
            copy(slot(peer, sub, 1 - c), 0, pair=1 - c).wait_recv()
    for one in sent:
        one.wait_send()


def norm_rows(values):
    row_mean = jnp.mean(values, axis=-1, keepdims=True)
    centred = values - row_mean
    row_var = jnp.mean(centred * centred, axis=-1, keepdims=True)
    scale = lax.rsqrt(row_var + epsilon)
    return centred * scale, scale


def norm_rows_back(unit, scale, cotangent):
    first = jnp.mean(cotangent, axis=-1, keepdims=True)
    second = jnp.mean(cotangent * unit, axis=-1, keepdims=True)
    return scale * (cotangent - first - unit * second)


def sigmoid(values):
    return 0.5 * jnp.tanh(0.5 * values) + 0.5


def dot_nn(a, b):
    return lax.dot_general(a, b, (((1,), (0,)), ((), ())), preferred_element_type=F32)


def dot_nt(a, b):
    return lax.dot_general(a, b, (((1,), (1,)), ((), ())), preferred_element_type=F32)


def dot_tn(a, b):
    return lax.dot_general(a, b, (((0,), (0,)), ((), ())), preferred_element_type=F32)


def triangle(out, entry, table, length, block=4):
    def step(at, carry):
        totals = [None] * block
        for s in range(length):
            rows = table[s]
            for q in range(block):
                term = entry(at * block + q, s) * rows
                totals[q] = term if s == 0 else totals[q] + term
        for q in range(block):
            out[at * block + q] = totals[q]
        return carry

    lax.fori_loop(0, length // block, step, 0)


def crop_kernel(
    sizes, row_block, col_block,
    mask_ref, all_ref, w_proj_ref, w_gate_ref, w_out_ref, pair_own_ref,
    turned_ref, d_pair_ref, g_proj_ref, g_gate_ref, g_out_ref,
    mask, pair, gate, left, right, right_flat, right_by_k, cot_flat, d_up, crossed,
    d_cross, d_left, d_right, d_gate, up_flat, l_one, l_two, r_one, r_two,
    normed, d_proj, d_gate_b,
):
    rows, subs, pairs = sizes
    col_groups = subs * pairs
    length = rows * row_block
    half = row_block * col_block
    band = row_block * length
    r = lax.axis_index("row")
    cg = lax.axis_index("sub") * pairs + lax.axis_index("pair")
    width = w_gate_ref.shape[0]

    def get(ref, at):
        return jnp.concatenate(
            [
                ref[pl.ds(at * row_block, row_block), g * col_block : (g + 1) * col_block].reshape(half, width)
                for g in range(col_groups)
            ],
            axis=0,
        )

    def put(ref, at, values):
        for g in range(col_groups):
            ref[pl.ds(at * row_block, row_block), g * col_block : (g + 1) * col_block] = values[
                g * half : (g + 1) * half
            ].reshape(row_block, col_block, width)

    place = lax.broadcasted_iota(jnp.int32, (length, width), 0)
    col_mask = jnp.zeros((length, width), F32)
    for i in range(length):
        col_mask = jnp.where(place == i, mask_ref[i].astype(F32), col_mask)
    for i in range(length):
        mask[i] = col_mask * mask_ref[i].astype(F32)

    def front(at, carry):
        rows_at = pl.ds(pl.multiple_of(at * band, band), band)
        held = all_ref[pl.ds(at * col_groups, col_groups)]
        x = held[:, :half].reshape(band, width).astype(F32)
        cot_flat[rows_at] = held[:, half:].reshape(band, width).astype(F32)
        put(pair, at, x)
        unit, _ = norm_rows(x)
        unit_b = unit.astype(BF16)
        normed[rows_at] = unit_b
        m = get(mask, at)
        put(gate, at, sigmoid(dot_nn(unit_b, w_gate_ref[...])))
        projected = dot_nn(unit_b, w_proj_ref[...])
        for base, ref, one, two in ((0, left, l_one, l_two), (2, right, r_one, r_two)):
            s = sigmoid(projected[:, base * width : (base + 1) * width])
            v = projected[:, (base + 1) * width : (base + 2) * width]
            sm = s * m
            vs = v * sm
            one[rows_at] = sm
            two[rows_at] = vs * (1.0 - s)
            put(ref, at, vs.astype(BF16).astype(F32))
        return carry

    lax.fori_loop(0, rows, front, 0)

    def spread(i, carry):
        right_flat[pl.ds(pl.multiple_of(i * length, length), length)] = right[i]
        return carry

    lax.fori_loop(0, length, spread, 0)
    for i in range(length):
        right_by_k[i] = right_flat[pl.ds(i, length, stride=length)]
        d_up[i] = cot_flat[pl.ds(i, length, stride=length)]

    triangle(crossed, lambda a, s: left[a, pl.ds(s, 1)], right_by_k, length)

    g_out_ref[...] = jnp.zeros_like(g_out_ref)
    g_proj_ref[...] = jnp.zeros_like(g_proj_ref)
    g_gate_ref[...] = jnp.zeros_like(g_gate_ref)

    def middle(at, carry):
        here = pl.ds(at * row_block, row_block)

        def flat(ref):
            return ref[here].reshape(band, width)

        unit, scale = norm_rows(flat(crossed).astype(BF16).astype(F32))
        unit_b = unit.astype(BF16)
        w_out = w_out_ref[...]
        out_proj = dot_nn(unit_b, w_out)
        g = flat(gate)
        up = flat(d_up)
        gated = g * out_proj
        up_flat[pl.ds(pl.multiple_of(at * band, band), band)] = flat(pair) + gated
        d_out_b = (g * up).astype(BF16)
        d_gate[here] = (gated * up * (1.0 - g)).reshape(row_block, length, width)
        d_unit = dot_nt(d_out_b, w_out)
        back = norm_rows_back(unit, scale, d_unit)
        d_cross[here] = back.astype(BF16).astype(F32).reshape(row_block, length, width)
        g_out_ref[...] += dot_tn(unit_b, d_out_b)
        return carry

    lax.fori_loop(0, rows, middle, 0)

    triangle(d_left, lambda a, s: d_cross[a, pl.ds(s, 1)], right, length)
    triangle(d_right, lambda a, s: d_cross[s, pl.ds(a, 1)], left, length)

    def finish(at, carry):
        rows_at = pl.ds(pl.multiple_of(at * band, band), band)
        dl, dr = get(d_left, at), get(d_right, at)
        parts = (dl * l_two[rows_at], dl * l_one[rows_at], dr * r_two[rows_at], dr * r_one[rows_at])
        unit_b = normed[rows_at]
        for q, part in enumerate(parts):
            part_b = part.astype(BF16)
            d_proj[rows_at, q * width : (q + 1) * width] = part_b
        g_proj_ref[...] += dot_tn(unit_b, d_proj[rows_at])
        gate_b = get(d_gate, at).astype(BF16)
        d_gate_b[rows_at] = gate_b
        g_gate_ref[...] += dot_tn(unit_b, gate_b)
        return carry

    lax.fori_loop(0, rows, finish, 0)

    share = 1.0 / length
    g_proj_ref[...] = g_proj_ref[...] * share
    g_gate_ref[...] = g_gate_ref[...] * share
    g_out_ref[...] = g_out_ref[...] * share

    own = r * col_groups + cg
    own_rows = pl.ds(pl.multiple_of(own * half, half), half)
    d_normed = dot_nt(d_proj[own_rows], w_proj_ref[...]) + dot_nt(d_gate_b[own_rows], w_gate_ref[...])
    unit, scale = norm_rows(pair_own_ref[...].astype(F32))
    up = d_up[
        pl.ds(r * row_block, row_block), pl.ds(pl.multiple_of(cg * col_block, col_block), col_block)
    ].reshape(half, width)
    d_pair_ref[...] = (up + norm_rows_back(unit, scale, d_normed)).astype(BF16)

    turned_rows = half // length
    for q in range(turned_rows):
        turned_ref[q * length : (q + 1) * length] = up_flat[
            pl.ds(own * turned_rows + q, length, stride=length)
        ].astype(BF16)


def on_device_whole(sizes, pair_act, residue_mask, w_proj, w_gate, w_out, d_transposed):
    row_block, col_block, channels = pair_act.shape
    rows, subs, pairs = sizes
    devices = rows * subs * pairs
    length = rows * row_block
    half = row_block * col_block
    pair_own = pair_act.reshape(half, channels)
    cot_own = d_transposed.reshape(half, channels)
    in_vmem = pl.BlockSpec(memory_space=pltpu.VMEM)
    everything = pl.pallas_call(
        functools.partial(gather_kernel, sizes),
        out_shape=jax.ShapeDtypeStruct((devices, 2 * half, channels), BF16),
        in_specs=[in_vmem] * 2,
        out_specs=in_vmem,
        scratch_shapes=[
            pltpu.SemaphoreType.DMA((devices,)),
            pltpu.SemaphoreType.DMA((devices,)),
        ],
        compiler_params=pltpu.CompilerParams(collective_id=0, has_side_effects=True),
        name="gather",
    )(pair_own, cot_own)
    cube = pltpu.VMEM((length, length, channels), F32)
    flat = pltpu.VMEM((length * length, channels), F32)
    turned, d_pair, g_proj, g_gate, g_out = pl.pallas_call(
        functools.partial(crop_kernel, sizes, row_block, col_block),
        out_shape=(
            jax.ShapeDtypeStruct((half, channels), BF16),
            jax.ShapeDtypeStruct((half, channels), BF16),
            jax.ShapeDtypeStruct(w_proj.shape, F32),
            jax.ShapeDtypeStruct(w_gate.shape, F32),
            jax.ShapeDtypeStruct(w_out.shape, F32),
        ),
        in_specs=[pl.BlockSpec(memory_space=pltpu.SMEM)] + [in_vmem] * 5,
        out_specs=[in_vmem] * 5,
        scratch_shapes=[
            cube, cube, cube, cube, cube, flat, cube, flat, cube, cube,
            cube, cube, cube, cube, flat, flat, flat, flat, flat,
            pltpu.VMEM((length * length, channels), BF16),
            pltpu.VMEM((length * length, w_proj.shape[1]), BF16),
            pltpu.VMEM((length * length, channels), BF16),
        ],
        compiler_params=pltpu.CompilerParams(vmem_limit_bytes=40 * 1024 * 1024),
        name="crop",
    )(residue_mask, everything, w_proj, w_gate, w_out, pair_own)
    return (
        turned.reshape(d_transposed.shape),
        d_pair.reshape(pair_act.shape),
        g_proj,
        g_gate,
        g_out,
    )


def choose(sizes, pair_act, residue_mask, w_proj, w_gate, w_out, d_transposed):
    row_block, col_block, channels = pair_act.shape
    length = sizes[0] * row_block
    fits = (
        length <= 32
        and row_block % 8 == 0
        and col_block % 8 == 0
        and sizes[1:] == (2, 2)
        and w_out.shape == (128, 128)
        and w_proj.shape == (128, 512)
    )
    body = functools.partial(on_device_whole, sizes) if fits else on_device
    return body(pair_act, residue_mask, w_proj, w_gate, w_out, d_transposed)


def solution(mesh):
    in_specs = (
        P(("crops", "row"), ("sub", "pair"), None),
        P("crops"),
        P(),
        P(),
        P(),
        P(("crops", "row", "sub", "pair"), None, None),
    )
    out_specs = (
        P(("crops", "row", "sub", "pair"), None, None),
        P(("crops", "row"), ("sub", "pair"), None),
        P("crops", None),
        P("crops", None),
        P("crops", None),
    )
    sizes = (mesh.shape["row"], mesh.shape["sub"], mesh.shape["pair"])
    return jax.shard_map(
        functools.partial(choose, sizes), mesh=mesh, in_specs=in_specs, out_specs=out_specs, check_vma=False
    )
```

```python
import functools

import jax
import jax.numpy as jnp
from jax import lax
from jax.experimental import pallas as pl
from jax.experimental.pallas import tpu as pltpu
from jax.sharding import PartitionSpec as P

epsilon = 1e-05


def layer_norm(values):
    row_mean = jnp.mean(values, axis=-1, keepdims=True)
    centred = values - row_mean
    row_var = jnp.mean(centred * centred, axis=-1, keepdims=True)
    return centred * lax.rsqrt(row_var + epsilon)


def norm_back(values, cotangent):
    return jax.vjp(layer_norm, values)[1](cotangent)[0]


def front_forward(pair_rows, w_proj, w_gate, pair_mask):
    hidden_width = w_proj.shape[1] // 4
    normed = layer_norm(pair_rows).astype(jnp.bfloat16)
    projected = jnp.dot(normed, w_proj, preferred_element_type=jnp.float32)
    gate_pre = jnp.dot(normed, w_gate, preferred_element_type=jnp.float32)
    left_b = (
        jax.nn.sigmoid(projected[:, :hidden_width])
        * projected[:, hidden_width : 2 * hidden_width]
        * pair_mask
    )
    right_b = (
        jax.nn.sigmoid(projected[:, 2 * hidden_width : 3 * hidden_width])
        * projected[:, 3 * hidden_width :]
        * pair_mask
    )
    return (
        normed,
        projected,
        left_b.astype(jnp.bfloat16),
        right_b.astype(jnp.bfloat16),
        jax.nn.sigmoid(gate_pre),
    )


def back_forward(crossed_rows, gate_act, pair_rows, w_out):
    normed_x = layer_norm(crossed_rows.astype(jnp.float32)).astype(jnp.bfloat16)
    out_proj = jnp.dot(normed_x, w_out, preferred_element_type=jnp.float32)
    return (normed_x, out_proj, pair_rows + gate_act * out_proj)


def back_backward(crossed_rows, out_proj, gate_act, w_out, d_up):
    d_out_b = (gate_act * d_up).astype(jnp.bfloat16)
    d_gate_b = (out_proj * d_up * gate_act * (1.0 - gate_act)).astype(jnp.bfloat16)
    d_normed_x = jnp.dot(d_out_b, w_out.T, preferred_element_type=jnp.float32)
    d_cross_b = norm_back(crossed_rows.astype(jnp.float32), d_normed_x).astype(jnp.bfloat16)
    return (d_out_b, d_gate_b, d_cross_b)


def front_backward(
    pair_rows, projected, pair_mask, d_left, d_right, d_gate_b, w_proj, w_gate, d_up
):
    hidden_width = w_proj.shape[1] // 4
    left_gate = jax.nn.sigmoid(projected[:, :hidden_width])
    left_value = projected[:, hidden_width : 2 * hidden_width]
    right_gate = jax.nn.sigmoid(projected[:, 2 * hidden_width : 3 * hidden_width])
    right_value = projected[:, 3 * hidden_width :]
    d_proj = jnp.concatenate(
        [
            d_left * left_value * pair_mask * left_gate * (1.0 - left_gate),
            d_left * left_gate * pair_mask,
            d_right * right_value * pair_mask * right_gate * (1.0 - right_gate),
            d_right * right_gate * pair_mask,
        ],
        axis=1,
    ).astype(jnp.bfloat16)
    d_normed = jnp.dot(d_proj, w_proj.T, preferred_element_type=jnp.float32) + jnp.dot(
        d_gate_b, w_gate.T, preferred_element_type=jnp.float32
    )
    d_pair = (d_up + norm_back(pair_rows, d_normed)).astype(jnp.bfloat16)
    return (d_proj, d_pair)


def to_channels(stacked, row_block, col_block):
    groups = stacked.shape[0]
    col_groups = lax.axis_size(("sub", "pair"))
    sectioning = stacked[None]
    arrived = lax.all_to_all(sectioning, ("sub", "pair"), split_axis=2, concat_axis=0, tiled=True)
    channel_share = arrived.shape[2]
    arrived = arrived.reshape(col_groups, groups, channel_share, row_block, col_block)
    return arrived.transpose(1, 2, 3, 0, 4).reshape(
        groups, channel_share, row_block, col_groups * col_block
    )


def from_channels(stacked, row_block, col_block):
    groups = stacked.shape[0]
    arrived = lax.all_to_all(stacked, ("sub", "pair"), split_axis=3, concat_axis=1, tiled=True)
    return arrived.transpose(0, 2, 3, 1).reshape(groups, row_block * col_block, arrived.shape[1])


def on_device(pair_act, residue_mask, w_proj, w_gate, w_out, d_transposed):
    row_block, col_block, channels = pair_act.shape
    row_count = lax.axis_size("row")
    col_groups = lax.axis_size(("sub", "pair"))
    crop_length = row_block * row_count
    block_width = col_block // row_count
    group_width = row_count // col_groups
    local_rows = row_block * col_block
    row_start = lax.axis_index("row") * row_block
    col_start = lax.axis_index(("sub", "pair")) * col_block
    row_valid = lax.dynamic_slice_in_dim(residue_mask, row_start, row_block, 0).astype(jnp.float32)
    col_valid = lax.dynamic_slice_in_dim(residue_mask, col_start, col_block, 0).astype(jnp.float32)
    pair_mask = (row_valid[:, None] * col_valid[None, :]).reshape(local_rows, 1)
    pair_rows = pair_act.reshape(local_rows, channels).astype(jnp.float32)
    normed, projected, left_b, right_b, gate_act = front_forward(
        pair_rows, w_proj, w_gate, pair_mask
    )
    paired = to_channels(jnp.stack([left_b.T, right_b.T]), row_block, col_block)
    left_t = paired[0]
    right_t = paired[1]
    crossed = jnp.einsum(
        "cik,cjk->cij",
        left_t,
        lax.all_gather(right_t, "row", axis=1, tiled=True),
        preferred_element_type=jnp.float32,
    )
    crossed_rows = from_channels(crossed.astype(jnp.bfloat16)[None], row_block, col_block)[0]
    normed_x, out_proj, updated = back_forward(crossed_rows, gate_act, pair_rows, w_out)
    updated_b = updated.astype(jnp.bfloat16).reshape(
        row_block, group_width, col_groups, block_width, channels
    )
    spread_cols = lax.all_to_all(
        updated_b, ("sub", "pair"), split_axis=2, concat_axis=2, tiled=True
    )
    regrouped = spread_cols.transpose(2, 1, 0, 3, 4).reshape(
        row_count, row_block, block_width, channels
    )
    turned = lax.all_to_all(regrouped, "row", split_axis=0, concat_axis=1, tiled=True)
    transposed = turned.reshape(crop_length, block_width, channels).transpose(1, 0, 2)
    back_in = d_transposed.transpose(1, 0, 2).reshape(row_count, row_block, block_width, channels)
    returned = lax.all_to_all(back_in, "row", split_axis=0, concat_axis=0, tiled=True)
    regrouped_back = returned.reshape(
        col_groups, group_width, row_block, block_width, channels
    ).transpose(2, 1, 0, 3, 4)
    restored = lax.all_to_all(
        regrouped_back, ("sub", "pair"), split_axis=2, concat_axis=2, tiled=True
    )
    d_up = restored.reshape(local_rows, channels).astype(jnp.float32)
    d_out_b, d_gate_b, d_cross_b = back_backward(crossed_rows, out_proj, gate_act, w_out, d_up)
    d_cross_t = to_channels(d_cross_b.T[None], row_block, col_block)[0]
    d_cross_cols = lax.all_to_all(d_cross_t, "row", split_axis=2, concat_axis=1, tiled=True)
    left_part = jnp.einsum(
        "cij,cjk->cik",
        d_cross_t,
        lax.all_gather(right_t, "row", axis=1, tiled=True),
        preferred_element_type=jnp.float32,
    )
    right_part = jnp.einsum(
        "cij,cik->cjk",
        d_cross_cols,
        lax.all_gather(left_t, "row", axis=1, tiled=True),
        preferred_element_type=jnp.float32,
    )
    d_rows_back = from_channels(
        jnp.stack([left_part, right_part]).astype(jnp.bfloat16), row_block, col_block
    )
    d_proj, d_pair = front_backward(
        pair_rows,
        projected,
        pair_mask,
        d_rows_back[0].astype(jnp.float32),
        d_rows_back[1].astype(jnp.float32),
        d_gate_b,
        w_proj,
        w_gate,
        d_up,
    )
    weight_terms = (
        jnp.einsum("rc,rd->cd", normed, d_proj, preferred_element_type=jnp.float32),
        jnp.einsum("rc,rd->cd", normed, d_gate_b, preferred_element_type=jnp.float32),
        jnp.einsum("rc,rd->cd", normed_x, d_out_b, preferred_element_type=jnp.float32),
    )
    g_proj, g_gate, g_out = lax.psum(
        (weight_terms[0], weight_terms[1], weight_terms[2]), ("row", "sub", "pair")
    )
    return (
        transposed,
        d_pair.reshape(row_block, col_block, channels),
        g_proj / crop_length,
        g_gate / crop_length,
        g_out / crop_length,
    )


MESH = pl.DeviceIdType.MESH
F32 = jnp.float32
BF16 = jnp.bfloat16


def norm_rows(values):
    row_mean = jnp.mean(values, axis=-1, keepdims=True)
    centred = values - row_mean
    row_var = jnp.mean(centred * centred, axis=-1, keepdims=True)
    scale = lax.rsqrt(row_var + epsilon)
    return centred * scale, scale


def norm_rows_back(unit, scale, cotangent):
    first = jnp.mean(cotangent, axis=-1, keepdims=True)
    second = jnp.mean(cotangent * unit, axis=-1, keepdims=True)
    return scale * (cotangent - first - unit * second)


def sigmoid(values):
    return 0.5 * jnp.tanh(0.5 * values) + 0.5


def dot_nn(a, b):
    return lax.dot_general(a, b, (((1,), (0,)), ((), ())), preferred_element_type=F32)


def dot_nt(a, b):
    return lax.dot_general(a, b, (((1,), (1,)), ((), ())), preferred_element_type=F32)


def dot_tn(a, b):
    return lax.dot_general(a, b, (((0,), (0,)), ((), ())), preferred_element_type=F32)


def triangle(out, entry, table, length, block=4):
    def step(at, carry):
        totals = [None] * block
        for s in range(length):
            rows = table[s]
            for q in range(block):
                term = entry(at * block + q, s) * rows
                totals[q] = term if s == 0 else totals[q] + term
        for q in range(block):
            out[at * block + q] = totals[q]
        return carry

    lax.fori_loop(0, length // block, step, 0)


def get(ref, at, sizes, shape):
    row_block, col_block, width = shape
    return jnp.concatenate(
        [
            ref[pl.ds(at * row_block, row_block), g * col_block : (g + 1) * col_block].reshape(
                row_block * col_block, width
            )
            for g in range(sizes[1] * sizes[2])
        ],
        axis=0,
    )


def put(ref, at, sizes, shape, values):
    row_block, col_block, width = shape
    half = row_block * col_block
    for g in range(sizes[1] * sizes[2]):
        ref[pl.ds(at * row_block, row_block), g * col_block : (g + 1) * col_block] = values[
            g * half : (g + 1) * half
        ].reshape(row_block, col_block, width)


def front_kernel(
    sizes, shape,
    pair_hbm, cot_hbm, mask_hbm, w_proj_hbm, w_gate_hbm,
    cot_all, pair, gate, left, right, l_one, l_two, r_one, r_two, normed,
    pair_all, w_proj, w_gate, mask_row, mask, own_sem, send_sem, recv_sem,
):
    rows, subs, pairs = sizes
    row_block, col_block, width = shape
    col_groups = subs * pairs
    length = rows * row_block
    half = row_block * col_block
    band = row_block * length
    r, x, c = lax.axis_index("row"), lax.axis_index("sub"), lax.axis_index("pair")

    def slot(row, sub, pair_at):
        return (row * subs + sub) * pairs + pair_at

    me = slot(r, x, c)
    if rows == 4:
        order = [r, r + 1 - 2 * (r % 2), r + 2 - 4 * (r // 2), 3 - r]
    else:
        order = [(r + step) % rows for step in range(rows)]
    far_first = [(order[q], sub) for q in reversed(range(1, rows)) for sub in (1 - x, x)] + [(r, 1 - x)]

    local = [
        pltpu.make_async_copy(pair_hbm, pair_all.at[me], own_sem.at[0]),
        pltpu.make_async_copy(cot_hbm, cot_all.at[me], own_sem.at[1]),
        pltpu.make_async_copy(mask_hbm, mask_row, own_sem.at[2]),
        pltpu.make_async_copy(w_proj_hbm, w_proj, own_sem.at[3]),
        pltpu.make_async_copy(w_gate_hbm, w_gate, own_sem.at[4]),
    ]
    for one in local:
        one.start()

    barrier = pltpu.get_barrier_semaphore()
    for row, sub in far_first:
        pl.semaphore_signal(barrier, inc=1, device_id={"row": row, "sub": sub}, device_id_type=MESH)
    pl.semaphore_signal(barrier, inc=1, device_id={"pair": 1 - c}, device_id_type=MESH)

    local[2].wait()
    place = lax.broadcasted_iota(jnp.int32, (length, width), 0)
    col_mask = jnp.zeros((length, width), F32)
    for i in range(length):
        col_mask = jnp.where(place == i, mask_row[i].astype(F32), col_mask)
    for i in range(length):
        mask[i] = col_mask * mask_row[i].astype(F32)
    for one in (local[0], local[1], local[3], local[4]):
        one.wait()
    pl.semaphore_wait(barrier, len(far_first) + 1)

    buffers = (pair_all, cot_all)
    sent = ([], [])

    def copy(kind, owner, number, target):
        return pltpu.make_async_remote_copy(
            src_ref=buffers[kind].at[owner],
            dst_ref=buffers[kind].at[owner],
            send_sem=send_sem.at[kind, number],
            recv_sem=recv_sem.at[kind, owner],
            device_id=target,
            device_id_type=MESH,
        )

    def send(kind, owner, target):
        one = copy(kind, owner, len(sent[kind]), target)
        one.start()
        sent[kind].append(one)

    other = {"pair": 1 - c}

    def send_own(kind):
        for row, sub in far_first:
            send(kind, me, {"row": row, "sub": sub})
        send(kind, me, other)

    def pass_on(kind, q):
        for sub in (1 - x,) if q == 0 else (x, 1 - x):
            owner = slot(order[q], sub, c)
            copy(kind, owner, 0, other).wait_recv()
            send(kind, owner, other)

    def from_other(kind, q):
        for sub in (x, 1 - x):
            copy(kind, slot(order[q], sub, 1 - c), 0, other).wait_recv()

    def front(q):
        at = order[q]
        rows_at = pl.ds(pl.multiple_of(at * band, band), band)
        values = pair_all[pl.ds(at * col_groups, col_groups)].reshape(band, width).astype(F32)
        put(pair, at, sizes, shape, values)
        unit, _ = norm_rows(values)
        unit_b = unit.astype(BF16)
        normed[rows_at] = unit_b
        m = get(mask, at, sizes, shape)
        put(gate, at, sizes, shape, sigmoid(dot_nn(unit_b, w_gate[...])))
        projected = dot_nn(unit_b, w_proj[...])
        for base, ref, one, two in ((0, left, l_one, l_two), (2, right, r_one, r_two)):
            s = sigmoid(projected[:, base * width : (base + 1) * width])
            v = projected[:, (base + 1) * width : (base + 2) * width]
            sm = s * m
            vs = v * sm
            one[rows_at] = sm
            two[rows_at] = vs * (1.0 - s)
            put(ref, at, sizes, shape, vs.astype(BF16).astype(F32))

    send_own(0)
    send_own(1)
    pass_on(0, 0)
    pass_on(0, 1)
    from_other(0, 0)
    front(0)
    for q in range(2, rows):
        pass_on(0, q)
    pass_on(1, 0)
    for q in range(1, rows):
        from_other(0, q)
        front(q)
        pass_on(1, q)
    for q in range(rows):
        from_other(1, q)
    for kind in (0, 1):
        for one in sent[kind]:
            one.wait_send()


def crop_kernel(
    sizes, shape,
    cot_all, pair, gate, left, right, l_one, l_two, r_one, r_two, normed,
    w_proj_ref, w_gate_ref, w_out_ref, pair_own_ref,
    turned_ref, d_pair_ref, g_proj_ref, g_gate_ref, g_out_ref,
    right_by_k, cot_flat, d_up, crossed,
    d_cross, d_left, d_right, d_gate, up_flat, d_proj, d_gate_b,
):
    rows, subs, pairs = sizes
    row_block, col_block, width = shape
    col_groups = subs * pairs
    length = rows * row_block
    half = row_block * col_block
    band = row_block * length
    r = lax.axis_index("row")
    cg = lax.axis_index("sub") * pairs + lax.axis_index("pair")

    cot_flat[...] = cot_all[...].reshape(length * length, width).astype(F32)
    right_flat = right.reshape(length * length, width)
    for i in range(length):
        right_by_k[i] = right_flat[pl.ds(i, length, stride=length)]
        d_up[i] = cot_flat[pl.ds(i, length, stride=length)]

    triangle(crossed, lambda a, s: left[a, pl.ds(s, 1)], right_by_k, length)

    g_out_ref[...] = jnp.zeros_like(g_out_ref)
    g_proj_ref[...] = jnp.zeros_like(g_proj_ref)
    g_gate_ref[...] = jnp.zeros_like(g_gate_ref)

    def middle(at, carry):
        here = pl.ds(at * row_block, row_block)

        def flat(ref):
            return ref[here].reshape(band, width)

        unit, scale = norm_rows(flat(crossed).astype(BF16).astype(F32))
        unit_b = unit.astype(BF16)
        w_out = w_out_ref[...]
        out_proj = dot_nn(unit_b, w_out)
        g = flat(gate)
        up = flat(d_up)
        gated = g * out_proj
        up_flat[pl.ds(pl.multiple_of(at * band, band), band)] = flat(pair) + gated
        d_out_b = (g * up).astype(BF16)
        d_gate[here] = (gated * up * (1.0 - g)).reshape(row_block, length, width)
        d_unit = dot_nt(d_out_b, w_out)
        back = norm_rows_back(unit, scale, d_unit)
        d_cross[here] = back.astype(BF16).astype(F32).reshape(row_block, length, width)
        g_out_ref[...] += dot_tn(unit_b, d_out_b)
        return carry

    lax.fori_loop(0, rows, middle, 0)

    triangle(d_left, lambda a, s: d_cross[a, pl.ds(s, 1)], right, length)
    triangle(d_right, lambda a, s: d_cross[s, pl.ds(a, 1)], left, length)

    def finish(at, carry):
        rows_at = pl.ds(pl.multiple_of(at * band, band), band)
        dl, dr = get(d_left, at, sizes, shape), get(d_right, at, sizes, shape)
        parts = (dl * l_two[rows_at], dl * l_one[rows_at], dr * r_two[rows_at], dr * r_one[rows_at])
        unit_b = normed[rows_at]
        for q, part in enumerate(parts):
            part_b = part.astype(BF16)
            d_proj[rows_at, q * width : (q + 1) * width] = part_b
        g_proj_ref[...] += dot_tn(unit_b, d_proj[rows_at])
        gate_b = get(d_gate, at, sizes, shape).astype(BF16)
        d_gate_b[rows_at] = gate_b
        g_gate_ref[...] += dot_tn(unit_b, gate_b)
        return carry

    lax.fori_loop(0, rows, finish, 0)

    share = 1.0 / length
    g_proj_ref[...] = g_proj_ref[...] * share
    g_gate_ref[...] = g_gate_ref[...] * share
    g_out_ref[...] = g_out_ref[...] * share

    own = r * col_groups + cg
    own_rows = pl.ds(pl.multiple_of(own * half, half), half)
    d_normed = dot_nt(d_proj[own_rows], w_proj_ref[...]) + dot_nt(d_gate_b[own_rows], w_gate_ref[...])
    unit, scale = norm_rows(pair_own_ref[...].astype(F32))
    up = d_up[
        pl.ds(r * row_block, row_block), pl.ds(pl.multiple_of(cg * col_block, col_block), col_block)
    ].reshape(half, width)
    d_pair_ref[...] = (up + norm_rows_back(unit, scale, d_normed)).astype(BF16)

    turned_rows = half // length
    for q in range(turned_rows):
        turned_ref[q * length : (q + 1) * length] = up_flat[
            pl.ds(own * turned_rows + q, length, stride=length)
        ].astype(BF16)


def on_device_whole(sizes, pair_act, residue_mask, w_proj, w_gate, w_out, d_transposed):
    row_block, col_block, channels = pair_act.shape
    rows, subs, pairs = sizes
    devices = rows * subs * pairs
    length = rows * row_block
    half = row_block * col_block
    pair_own = pair_act.reshape(half, channels)
    cot_own = d_transposed.reshape(half, channels)
    shape = (row_block, col_block, channels)
    in_vmem = pl.BlockSpec(memory_space=pltpu.VMEM)
    in_hbm = pl.BlockSpec(memory_space=pltpu.HBM)
    cube = (length, length, channels)
    flat = (length * length, channels)
    kept = [jax.ShapeDtypeStruct(cube, F32)] * 4 + [jax.ShapeDtypeStruct(flat, F32)] * 4
    held = pl.pallas_call(
        functools.partial(front_kernel, sizes, shape),
        out_shape=[
            jax.ShapeDtypeStruct((devices, half, channels), BF16),
            *kept,
            jax.ShapeDtypeStruct(flat, BF16),
        ],
        in_specs=[in_hbm] * 5,
        out_specs=[in_vmem] * 10,
        scratch_shapes=[
            pltpu.VMEM((devices, half, channels), BF16),
            pltpu.VMEM(w_proj.shape, BF16),
            pltpu.VMEM(w_gate.shape, BF16),
            pltpu.SMEM((length,), jnp.int32),
            pltpu.VMEM(cube, F32),
            pltpu.SemaphoreType.DMA((5,)),
            pltpu.SemaphoreType.DMA((2, devices)),
            pltpu.SemaphoreType.DMA((2, devices)),
        ],
        compiler_params=pltpu.CompilerParams(
            collective_id=0, has_side_effects=True, vmem_limit_bytes=16 * 1024 * 1024
        ),
        name="front",
    )(pair_own, cot_own, residue_mask, w_proj, w_gate)
    cube_room = pltpu.VMEM(cube, F32)
    flat_room = pltpu.VMEM(flat, F32)
    turned, d_pair, g_proj, g_gate, g_out = pl.pallas_call(
        functools.partial(crop_kernel, sizes, shape),
        out_shape=(
            jax.ShapeDtypeStruct((half, channels), BF16),
            jax.ShapeDtypeStruct((half, channels), BF16),
            jax.ShapeDtypeStruct(w_proj.shape, F32),
            jax.ShapeDtypeStruct(w_gate.shape, F32),
            jax.ShapeDtypeStruct(w_out.shape, F32),
        ),
        in_specs=[in_vmem] * 14,
        out_specs=[in_vmem] * 5,
        scratch_shapes=[
            cube_room, flat_room, cube_room, cube_room,
            cube_room, cube_room, cube_room, cube_room, flat_room,
            pltpu.VMEM((length * length, w_proj.shape[1]), BF16),
            pltpu.VMEM(flat, BF16),
        ],
        compiler_params=pltpu.CompilerParams(vmem_limit_bytes=24 * 1024 * 1024),
        name="crop",
    )(*held, w_proj, w_gate, w_out, pair_own)
    return (
        turned.reshape(d_transposed.shape),
        d_pair.reshape(pair_act.shape),
        g_proj,
        g_gate,
        g_out,
    )


def choose(sizes, pair_act, residue_mask, w_proj, w_gate, w_out, d_transposed):
    row_block, col_block, channels = pair_act.shape
    length = sizes[0] * row_block
    fits = (
        length <= 32
        and row_block % 8 == 0
        and col_block % 8 == 0
        and sizes[1:] == (2, 2)
        and w_out.shape == (128, 128)
        and w_proj.shape == (128, 512)
    )
    body = functools.partial(on_device_whole, sizes) if fits else on_device
    return body(pair_act, residue_mask, w_proj, w_gate, w_out, d_transposed)


def solution(mesh):
    in_specs = (
        P(("crops", "row"), ("sub", "pair"), None),
        P("crops"),
        P(),
        P(),
        P(),
        P(("crops", "row", "sub", "pair"), None, None),
    )
    out_specs = (
        P(("crops", "row", "sub", "pair"), None, None),
        P(("crops", "row"), ("sub", "pair"), None),
        P("crops", None),
        P("crops", None),
        P("crops", None),
    )
    sizes = (mesh.shape["row"], mesh.shape["sub"], mesh.shape["pair"])
    return jax.shard_map(
        functools.partial(choose, sizes), mesh=mesh, in_specs=in_specs, out_specs=out_specs, check_vma=False
    )
```

```python
import functools

import jax
import jax.numpy as jnp
from jax import lax
from jax.experimental import pallas as pl
from jax.experimental.pallas import tpu as pltpu
from jax.sharding import PartitionSpec as P

epsilon = 1e-05


def layer_norm(values):
    row_mean = jnp.mean(values, axis=-1, keepdims=True)
    centred = values - row_mean
    row_var = jnp.mean(centred * centred, axis=-1, keepdims=True)
    return centred * lax.rsqrt(row_var + epsilon)


def norm_back(values, cotangent):
    return jax.vjp(layer_norm, values)[1](cotangent)[0]


def front_forward(pair_rows, w_proj, w_gate, pair_mask):
    hidden_width = w_proj.shape[1] // 4
    normed = layer_norm(pair_rows).astype(jnp.bfloat16)
    projected = jnp.dot(normed, w_proj, preferred_element_type=jnp.float32)
    gate_pre = jnp.dot(normed, w_gate, preferred_element_type=jnp.float32)
    left_b = (
        jax.nn.sigmoid(projected[:, :hidden_width])
        * projected[:, hidden_width : 2 * hidden_width]
        * pair_mask
    )
    right_b = (
        jax.nn.sigmoid(projected[:, 2 * hidden_width : 3 * hidden_width])
        * projected[:, 3 * hidden_width :]
        * pair_mask
    )
    return (
        normed,
        projected,
        left_b.astype(jnp.bfloat16),
        right_b.astype(jnp.bfloat16),
        jax.nn.sigmoid(gate_pre),
    )


def back_forward(crossed_rows, gate_act, pair_rows, w_out):
    normed_x = layer_norm(crossed_rows.astype(jnp.float32)).astype(jnp.bfloat16)
    out_proj = jnp.dot(normed_x, w_out, preferred_element_type=jnp.float32)
    return (normed_x, out_proj, pair_rows + gate_act * out_proj)


def back_backward(crossed_rows, out_proj, gate_act, w_out, d_up):
    d_out_b = (gate_act * d_up).astype(jnp.bfloat16)
    d_gate_b = (out_proj * d_up * gate_act * (1.0 - gate_act)).astype(jnp.bfloat16)
    d_normed_x = jnp.dot(d_out_b, w_out.T, preferred_element_type=jnp.float32)
    d_cross_b = norm_back(crossed_rows.astype(jnp.float32), d_normed_x).astype(jnp.bfloat16)
    return (d_out_b, d_gate_b, d_cross_b)


def front_backward(
    pair_rows, projected, pair_mask, d_left, d_right, d_gate_b, w_proj, w_gate, d_up
):
    hidden_width = w_proj.shape[1] // 4
    left_gate = jax.nn.sigmoid(projected[:, :hidden_width])
    left_value = projected[:, hidden_width : 2 * hidden_width]
    right_gate = jax.nn.sigmoid(projected[:, 2 * hidden_width : 3 * hidden_width])
    right_value = projected[:, 3 * hidden_width :]
    d_proj = jnp.concatenate(
        [
            d_left * left_value * pair_mask * left_gate * (1.0 - left_gate),
            d_left * left_gate * pair_mask,
            d_right * right_value * pair_mask * right_gate * (1.0 - right_gate),
            d_right * right_gate * pair_mask,
        ],
        axis=1,
    ).astype(jnp.bfloat16)
    d_normed = jnp.dot(d_proj, w_proj.T, preferred_element_type=jnp.float32) + jnp.dot(
        d_gate_b, w_gate.T, preferred_element_type=jnp.float32
    )
    d_pair = (d_up + norm_back(pair_rows, d_normed)).astype(jnp.bfloat16)
    return (d_proj, d_pair)


def to_channels(stacked, row_block, col_block):
    groups = stacked.shape[0]
    col_groups = lax.axis_size(("sub", "pair"))
    sectioning = stacked[None]
    arrived = lax.all_to_all(sectioning, ("sub", "pair"), split_axis=2, concat_axis=0, tiled=True)
    channel_share = arrived.shape[2]
    arrived = arrived.reshape(col_groups, groups, channel_share, row_block, col_block)
    return arrived.transpose(1, 2, 3, 0, 4).reshape(
        groups, channel_share, row_block, col_groups * col_block
    )


def from_channels(stacked, row_block, col_block):
    groups = stacked.shape[0]
    arrived = lax.all_to_all(stacked, ("sub", "pair"), split_axis=3, concat_axis=1, tiled=True)
    return arrived.transpose(0, 2, 3, 1).reshape(groups, row_block * col_block, arrived.shape[1])


def on_device(pair_act, residue_mask, w_proj, w_gate, w_out, d_transposed):
    row_block, col_block, channels = pair_act.shape
    row_count = lax.axis_size("row")
    col_groups = lax.axis_size(("sub", "pair"))
    crop_length = row_block * row_count
    block_width = col_block // row_count
    group_width = row_count // col_groups
    local_rows = row_block * col_block
    row_start = lax.axis_index("row") * row_block
    col_start = lax.axis_index(("sub", "pair")) * col_block
    row_valid = lax.dynamic_slice_in_dim(residue_mask, row_start, row_block, 0).astype(jnp.float32)
    col_valid = lax.dynamic_slice_in_dim(residue_mask, col_start, col_block, 0).astype(jnp.float32)
    pair_mask = (row_valid[:, None] * col_valid[None, :]).reshape(local_rows, 1)
    pair_rows = pair_act.reshape(local_rows, channels).astype(jnp.float32)
    normed, projected, left_b, right_b, gate_act = front_forward(
        pair_rows, w_proj, w_gate, pair_mask
    )
    paired = to_channels(jnp.stack([left_b.T, right_b.T]), row_block, col_block)
    left_t = paired[0]
    right_t = paired[1]
    crossed = jnp.einsum(
        "cik,cjk->cij",
        left_t,
        lax.all_gather(right_t, "row", axis=1, tiled=True),
        preferred_element_type=jnp.float32,
    )
    crossed_rows = from_channels(crossed.astype(jnp.bfloat16)[None], row_block, col_block)[0]
    normed_x, out_proj, updated = back_forward(crossed_rows, gate_act, pair_rows, w_out)
    updated_b = updated.astype(jnp.bfloat16).reshape(
        row_block, group_width, col_groups, block_width, channels
    )
    spread_cols = lax.all_to_all(
        updated_b, ("sub", "pair"), split_axis=2, concat_axis=2, tiled=True
    )
    regrouped = spread_cols.transpose(2, 1, 0, 3, 4).reshape(
        row_count, row_block, block_width, channels
    )
    turned = lax.all_to_all(regrouped, "row", split_axis=0, concat_axis=1, tiled=True)
    transposed = turned.reshape(crop_length, block_width, channels).transpose(1, 0, 2)
    back_in = d_transposed.transpose(1, 0, 2).reshape(row_count, row_block, block_width, channels)
    returned = lax.all_to_all(back_in, "row", split_axis=0, concat_axis=0, tiled=True)
    regrouped_back = returned.reshape(
        col_groups, group_width, row_block, block_width, channels
    ).transpose(2, 1, 0, 3, 4)
    restored = lax.all_to_all(
        regrouped_back, ("sub", "pair"), split_axis=2, concat_axis=2, tiled=True
    )
    d_up = restored.reshape(local_rows, channels).astype(jnp.float32)
    d_out_b, d_gate_b, d_cross_b = back_backward(crossed_rows, out_proj, gate_act, w_out, d_up)
    d_cross_t = to_channels(d_cross_b.T[None], row_block, col_block)[0]
    d_cross_cols = lax.all_to_all(d_cross_t, "row", split_axis=2, concat_axis=1, tiled=True)
    left_part = jnp.einsum(
        "cij,cjk->cik",
        d_cross_t,
        lax.all_gather(right_t, "row", axis=1, tiled=True),
        preferred_element_type=jnp.float32,
    )
    right_part = jnp.einsum(
        "cij,cik->cjk",
        d_cross_cols,
        lax.all_gather(left_t, "row", axis=1, tiled=True),
        preferred_element_type=jnp.float32,
    )
    d_rows_back = from_channels(
        jnp.stack([left_part, right_part]).astype(jnp.bfloat16), row_block, col_block
    )
    d_proj, d_pair = front_backward(
        pair_rows,
        projected,
        pair_mask,
        d_rows_back[0].astype(jnp.float32),
        d_rows_back[1].astype(jnp.float32),
        d_gate_b,
        w_proj,
        w_gate,
        d_up,
    )
    weight_terms = (
        jnp.einsum("rc,rd->cd", normed, d_proj, preferred_element_type=jnp.float32),
        jnp.einsum("rc,rd->cd", normed, d_gate_b, preferred_element_type=jnp.float32),
        jnp.einsum("rc,rd->cd", normed_x, d_out_b, preferred_element_type=jnp.float32),
    )
    g_proj, g_gate, g_out = lax.psum(
        (weight_terms[0], weight_terms[1], weight_terms[2]), ("row", "sub", "pair")
    )
    return (
        transposed,
        d_pair.reshape(row_block, col_block, channels),
        g_proj / crop_length,
        g_gate / crop_length,
        g_out / crop_length,
    )


MESH = pl.DeviceIdType.MESH
F32 = jnp.float32
BF16 = jnp.bfloat16


def norm_rows(values):
    row_mean = jnp.mean(values, axis=-1, keepdims=True)
    centred = values - row_mean
    row_var = jnp.mean(centred * centred, axis=-1, keepdims=True)
    scale = lax.rsqrt(row_var + epsilon)
    return centred * scale, scale


def norm_rows_back(unit, scale, cotangent):
    first = jnp.mean(cotangent, axis=-1, keepdims=True)
    second = jnp.mean(cotangent * unit, axis=-1, keepdims=True)
    return scale * (cotangent - first - unit * second)


def sigmoid(values):
    return 0.5 * jnp.tanh(0.5 * values) + 0.5


def dot_nn(a, b):
    return lax.dot_general(a, b, (((1,), (0,)), ((), ())), preferred_element_type=F32)


def dot_nt(a, b):
    return lax.dot_general(a, b, (((1,), (1,)), ((), ())), preferred_element_type=F32)


def dot_tn(a, b):
    return lax.dot_general(a, b, (((0,), (0,)), ((), ())), preferred_element_type=F32)


def triangle(out, entry, table, length, block=4, first=0, last=None):
    def step(at, carry):
        totals = [None] * block
        for s in range(length):
            rows = table[s]
            for q in range(block):
                term = entry(at * block + q, s) * rows
                totals[q] = term if s == 0 else totals[q] + term
        for q in range(block):
            out[at * block + q] = totals[q]
        return carry

    lax.fori_loop(first, length // block if last is None else last, step, 0)


def get(ref, at, sizes, shape):
    row_block, col_block, width = shape
    return jnp.concatenate(
        [
            ref[pl.ds(at * row_block, row_block), g * col_block : (g + 1) * col_block].reshape(
                row_block * col_block, width
            )
            for g in range(sizes[1] * sizes[2])
        ],
        axis=0,
    )


def put(ref, at, sizes, shape, values):
    row_block, col_block, width = shape
    half = row_block * col_block
    for g in range(sizes[1] * sizes[2]):
        ref[pl.ds(at * row_block, row_block), g * col_block : (g + 1) * col_block] = values[
            g * half : (g + 1) * half
        ].reshape(row_block, col_block, width)


def front_kernel(
    sizes, shape,
    pair_hbm, cot_hbm, mask_hbm, w_proj_hbm, w_gate_hbm,
    cot_all, pair, gate, left, right, crossed, l_one, l_two, r_one, r_two, normed,
    pair_all, right_by_k, w_proj, w_gate, mask_row, mask, own_sem, send_sem, recv_sem,
):
    rows, subs, pairs = sizes
    row_block, col_block, width = shape
    col_groups = subs * pairs
    length = rows * row_block
    half = row_block * col_block
    band = row_block * length
    r, x, c = lax.axis_index("row"), lax.axis_index("sub"), lax.axis_index("pair")

    def slot(row, sub, pair_at):
        return (row * subs + sub) * pairs + pair_at

    me = slot(r, x, c)
    if rows == 4:
        order = [r, r + 1 - 2 * (r % 2), r + 2 - 4 * (r // 2), 3 - r]
    else:
        order = [(r + step) % rows for step in range(rows)]
    far_first = [(order[q], sub) for q in reversed(range(1, rows)) for sub in (1 - x, x)] + [(r, 1 - x)]

    local = [
        pltpu.make_async_copy(pair_hbm, pair_all.at[me], own_sem.at[0]),
        pltpu.make_async_copy(cot_hbm, cot_all.at[me], own_sem.at[1]),
        pltpu.make_async_copy(mask_hbm, mask_row, own_sem.at[2]),
        pltpu.make_async_copy(w_proj_hbm, w_proj, own_sem.at[3]),
        pltpu.make_async_copy(w_gate_hbm, w_gate, own_sem.at[4]),
    ]
    for one in local:
        one.start()

    barrier = pltpu.get_barrier_semaphore()
    for row, sub in far_first:
        pl.semaphore_signal(barrier, inc=1, device_id={"row": row, "sub": sub}, device_id_type=MESH)
    pl.semaphore_signal(barrier, inc=1, device_id={"pair": 1 - c}, device_id_type=MESH)

    local[2].wait()
    place = lax.broadcasted_iota(jnp.int32, (length, width), 0)
    col_mask = jnp.zeros((length, width), F32)
    for i in range(length):
        col_mask = jnp.where(place == i, mask_row[i].astype(F32), col_mask)
    for i in range(length):
        mask[i] = col_mask * mask_row[i].astype(F32)
    for one in (local[0], local[1], local[3], local[4]):
        one.wait()
    pl.semaphore_wait(barrier, len(far_first) + 1)

    buffers = (pair_all, cot_all)
    sent = ([], [])

    def copy(kind, owner, number, target):
        return pltpu.make_async_remote_copy(
            src_ref=buffers[kind].at[owner],
            dst_ref=buffers[kind].at[owner],
            send_sem=send_sem.at[kind, number],
            recv_sem=recv_sem.at[kind, owner],
            device_id=target,
            device_id_type=MESH,
        )

    def send(kind, owner, target):
        one = copy(kind, owner, len(sent[kind]), target)
        one.start()
        sent[kind].append(one)

    other = {"pair": 1 - c}

    def send_own(kind):
        for row, sub in far_first:
            send(kind, me, {"row": row, "sub": sub})
        send(kind, me, other)

    def pass_on(kind, q):
        for sub in (1 - x,) if q == 0 else (x, 1 - x):
            owner = slot(order[q], sub, c)
            copy(kind, owner, 0, other).wait_recv()
            send(kind, owner, other)

    def from_other(kind, q):
        for sub in (x, 1 - x):
            copy(kind, slot(order[q], sub, 1 - c), 0, other).wait_recv()

    def front(q):
        at = order[q]
        rows_at = pl.ds(pl.multiple_of(at * band, band), band)
        values = pair_all[pl.ds(at * col_groups, col_groups)].reshape(band, width).astype(F32)
        put(pair, at, sizes, shape, values)
        unit, _ = norm_rows(values)
        unit_b = unit.astype(BF16)
        normed[rows_at] = unit_b
        m = get(mask, at, sizes, shape)
        put(gate, at, sizes, shape, sigmoid(dot_nn(unit_b, w_gate[...])))
        projected = dot_nn(unit_b, w_proj[...])
        for base, ref, one, two in ((0, left, l_one, l_two), (2, right, r_one, r_two)):
            s = sigmoid(projected[:, base * width : (base + 1) * width])
            v = projected[:, (base + 1) * width : (base + 2) * width]
            sm = s * m
            vs = v * sm
            one[rows_at] = sm
            two[rows_at] = vs * (1.0 - s)
            put(ref, at, sizes, shape, vs.astype(BF16).astype(F32))

    send_own(0)
    send_own(1)
    pass_on(0, 0)
    pass_on(0, 1)
    from_other(0, 0)
    front(0)
    for q in range(2, rows):
        pass_on(0, q)
    for q in range(1, rows):
        from_other(0, q)
        front(q)
    right_flat = right.reshape(length * length, width)
    for i in range(length):
        right_by_k[i] = right_flat[pl.ds(i, length, stride=length)]
    middle = length // 8
    pass_on(1, 0)
    pass_on(1, 1)
    triangle(crossed, lambda a, s: left[a, pl.ds(s, 1)], right_by_k, length, last=middle)
    for q in range(2, rows):
        pass_on(1, q)
    triangle(crossed, lambda a, s: left[a, pl.ds(s, 1)], right_by_k, length, first=middle)
    for q in range(rows):
        from_other(1, q)
    for kind in (0, 1):
        for one in sent[kind]:
            one.wait_send()


def crop_kernel(
    sizes, shape,
    cot_all, pair, gate, left, right, crossed, l_one, l_two, r_one, r_two, normed,
    w_proj_ref, w_gate_ref, w_out_ref,
    turned_ref, d_pair_ref, g_proj_ref, g_gate_ref, g_out_ref,
    cot_flat, d_up,
    d_cross, d_left, d_right, d_gate, up_flat, d_proj, d_gate_b,
):
    rows, subs, pairs = sizes
    row_block, col_block, width = shape
    col_groups = subs * pairs
    length = rows * row_block
    half = row_block * col_block
    band = row_block * length
    r = lax.axis_index("row")
    cg = lax.axis_index("sub") * pairs + lax.axis_index("pair")

    cot_flat[...] = cot_all[...].reshape(length * length, width).astype(F32)
    for i in range(length):
        d_up[i] = cot_flat[pl.ds(i, length, stride=length)]

    g_out_ref[...] = jnp.zeros_like(g_out_ref)
    g_proj_ref[...] = jnp.zeros_like(g_proj_ref)
    g_gate_ref[...] = jnp.zeros_like(g_gate_ref)

    def middle(at, carry):
        here = pl.ds(at * row_block, row_block)

        def flat(ref):
            return ref[here].reshape(band, width)

        unit, scale = norm_rows(flat(crossed).astype(BF16).astype(F32))
        unit_b = unit.astype(BF16)
        w_out = w_out_ref[...]
        out_proj = dot_nn(unit_b, w_out)
        g = flat(gate)
        up = flat(d_up)
        gated = g * out_proj
        up_flat[pl.ds(pl.multiple_of(at * band, band), band)] = flat(pair) + gated
        d_out_b = (g * up).astype(BF16)
        d_gate[here] = (gated * up * (1.0 - g)).reshape(row_block, length, width)
        d_unit = dot_nt(d_out_b, w_out)
        back = norm_rows_back(unit, scale, d_unit)
        d_cross[here] = back.astype(BF16).astype(F32).reshape(row_block, length, width)
        g_out_ref[...] += dot_tn(unit_b, d_out_b)
        return carry

    lax.fori_loop(0, rows, middle, 0)

    triangle(d_left, lambda a, s: d_cross[a, pl.ds(s, 1)], right, length)
    triangle(d_right, lambda a, s: d_cross[s, pl.ds(a, 1)], left, length)

    def finish(at, carry):
        rows_at = pl.ds(pl.multiple_of(at * band, band), band)
        dl, dr = get(d_left, at, sizes, shape), get(d_right, at, sizes, shape)
        parts = (dl * l_two[rows_at], dl * l_one[rows_at], dr * r_two[rows_at], dr * r_one[rows_at])
        unit_b = normed[rows_at]
        for q, part in enumerate(parts):
            part_b = part.astype(BF16)
            d_proj[rows_at, q * width : (q + 1) * width] = part_b
        g_proj_ref[...] += dot_tn(unit_b, d_proj[rows_at])
        gate_b = get(d_gate, at, sizes, shape).astype(BF16)
        d_gate_b[rows_at] = gate_b
        g_gate_ref[...] += dot_tn(unit_b, gate_b)
        return carry

    lax.fori_loop(0, rows, finish, 0)

    share = 1.0 / length
    g_proj_ref[...] = g_proj_ref[...] * share
    g_gate_ref[...] = g_gate_ref[...] * share
    g_out_ref[...] = g_out_ref[...] * share

    own = r * col_groups + cg
    own_rows = pl.ds(pl.multiple_of(own * half, half), half)
    d_normed = dot_nt(d_proj[own_rows], w_proj_ref[...]) + dot_nt(d_gate_b[own_rows], w_gate_ref[...])

    def own_block(ref):
        columns = pl.ds(pl.multiple_of(cg * col_block, col_block), col_block)
        return ref[pl.ds(r * row_block, row_block), columns].reshape(half, width)

    unit, scale = norm_rows(own_block(pair))
    up = own_block(d_up)
    d_pair_ref[...] = (up + norm_rows_back(unit, scale, d_normed)).astype(BF16)

    turned_rows = half // length
    for q in range(turned_rows):
        turned_ref[q * length : (q + 1) * length] = up_flat[
            pl.ds(own * turned_rows + q, length, stride=length)
        ].astype(BF16)


def on_device_whole(sizes, pair_act, residue_mask, w_proj, w_gate, w_out, d_transposed):
    row_block, col_block, channels = pair_act.shape
    rows, subs, pairs = sizes
    devices = rows * subs * pairs
    length = rows * row_block
    half = row_block * col_block
    pair_own = pair_act.reshape(half, channels)
    cot_own = d_transposed.reshape(half, channels)
    shape = (row_block, col_block, channels)
    in_vmem = pl.BlockSpec(memory_space=pltpu.VMEM)
    in_hbm = pl.BlockSpec(memory_space=pltpu.HBM)
    cube = (length, length, channels)
    flat = (length * length, channels)
    kept = [jax.ShapeDtypeStruct(cube, F32)] * 5 + [jax.ShapeDtypeStruct(flat, F32)] * 4
    held = pl.pallas_call(
        functools.partial(front_kernel, sizes, shape),
        out_shape=[
            jax.ShapeDtypeStruct((devices, half, channels), BF16),
            *kept,
            jax.ShapeDtypeStruct(flat, BF16),
        ],
        in_specs=[in_hbm] * 5,
        out_specs=[in_vmem] * 11,
        scratch_shapes=[
            pltpu.VMEM((devices, half, channels), BF16),
            pltpu.VMEM(cube, F32),
            pltpu.VMEM(w_proj.shape, BF16),
            pltpu.VMEM(w_gate.shape, BF16),
            pltpu.SMEM((length,), jnp.int32),
            pltpu.VMEM(cube, F32),
            pltpu.SemaphoreType.DMA((5,)),
            pltpu.SemaphoreType.DMA((2, devices)),
            pltpu.SemaphoreType.DMA((2, devices)),
        ],
        compiler_params=pltpu.CompilerParams(
            collective_id=0, has_side_effects=True, vmem_limit_bytes=16 * 1024 * 1024
        ),
        name="front",
    )(*(pltpu.with_memory_space_constraint(each, pltpu.HBM) for each in (pair_own, cot_own, residue_mask, w_proj, w_gate)))
    cube_room = pltpu.VMEM(cube, F32)
    flat_room = pltpu.VMEM(flat, F32)
    turned, d_pair, g_proj, g_gate, g_out = pl.pallas_call(
        functools.partial(crop_kernel, sizes, shape),
        out_shape=(
            jax.ShapeDtypeStruct((half, channels), BF16),
            jax.ShapeDtypeStruct((half, channels), BF16),
            jax.ShapeDtypeStruct(w_proj.shape, F32),
            jax.ShapeDtypeStruct(w_gate.shape, F32),
            jax.ShapeDtypeStruct(w_out.shape, F32),
        ),
        in_specs=[in_vmem] * 14,
        out_specs=[in_vmem] * 5,
        scratch_shapes=[
            flat_room, cube_room,
            cube_room, cube_room, cube_room, cube_room, flat_room,
            pltpu.VMEM((length * length, w_proj.shape[1]), BF16),
            pltpu.VMEM(flat, BF16),
        ],
        compiler_params=pltpu.CompilerParams(vmem_limit_bytes=24 * 1024 * 1024),
        name="crop",
    )(*held, w_proj, w_gate, w_out)
    return (
        turned.reshape(d_transposed.shape),
        d_pair.reshape(pair_act.shape),
        g_proj,
        g_gate,
        g_out,
    )


def choose(sizes, pair_act, residue_mask, w_proj, w_gate, w_out, d_transposed):
    row_block, col_block, channels = pair_act.shape
    length = sizes[0] * row_block
    fits = (
        length <= 32
        and row_block % 8 == 0
        and col_block % 8 == 0
        and sizes[1:] == (2, 2)
        and w_out.shape == (128, 128)
        and w_proj.shape == (128, 512)
    )
    body = functools.partial(on_device_whole, sizes) if fits else on_device
    return body(pair_act, residue_mask, w_proj, w_gate, w_out, d_transposed)


def solution(mesh):
    in_specs = (
        P(("crops", "row"), ("sub", "pair"), None),
        P("crops"),
        P(),
        P(),
        P(),
        P(("crops", "row", "sub", "pair"), None, None),
    )
    out_specs = (
        P(("crops", "row", "sub", "pair"), None, None),
        P(("crops", "row"), ("sub", "pair"), None),
        P("crops", None),
        P("crops", None),
        P("crops", None),
    )
    sizes = (mesh.shape["row"], mesh.shape["sub"], mesh.shape["pair"])
    return jax.shard_map(
        functools.partial(choose, sizes), mesh=mesh, in_specs=in_specs, out_specs=out_specs, check_vma=False
    )
```

```python
import functools

import jax
import jax.numpy as jnp
from jax import lax
from jax.experimental import pallas as pl
from jax.experimental.pallas import tpu as pltpu
from jax.sharding import PartitionSpec as P

epsilon = 1e-05


def layer_norm(values):
    row_mean = jnp.mean(values, axis=-1, keepdims=True)
    centred = values - row_mean
    row_var = jnp.mean(centred * centred, axis=-1, keepdims=True)
    return centred * lax.rsqrt(row_var + epsilon)


def norm_back(values, cotangent):
    return jax.vjp(layer_norm, values)[1](cotangent)[0]


def front_forward(pair_rows, w_proj, w_gate, pair_mask):
    hidden_width = w_proj.shape[1] // 4
    normed = layer_norm(pair_rows).astype(jnp.bfloat16)
    projected = jnp.dot(normed, w_proj, preferred_element_type=jnp.float32)
    gate_pre = jnp.dot(normed, w_gate, preferred_element_type=jnp.float32)
    left_b = (
        jax.nn.sigmoid(projected[:, :hidden_width])
        * projected[:, hidden_width : 2 * hidden_width]
        * pair_mask
    )
    right_b = (
        jax.nn.sigmoid(projected[:, 2 * hidden_width : 3 * hidden_width])
        * projected[:, 3 * hidden_width :]
        * pair_mask
    )
    return (
        normed,
        projected,
        left_b.astype(jnp.bfloat16),
        right_b.astype(jnp.bfloat16),
        jax.nn.sigmoid(gate_pre),
    )


def back_forward(crossed_rows, gate_act, pair_rows, w_out):
    normed_x = layer_norm(crossed_rows.astype(jnp.float32)).astype(jnp.bfloat16)
    out_proj = jnp.dot(normed_x, w_out, preferred_element_type=jnp.float32)
    return (normed_x, out_proj, pair_rows + gate_act * out_proj)


def back_backward(crossed_rows, out_proj, gate_act, w_out, d_up):
    d_out_b = (gate_act * d_up).astype(jnp.bfloat16)
    d_gate_b = (out_proj * d_up * gate_act * (1.0 - gate_act)).astype(jnp.bfloat16)
    d_normed_x = jnp.dot(d_out_b, w_out.T, preferred_element_type=jnp.float32)
    d_cross_b = norm_back(crossed_rows.astype(jnp.float32), d_normed_x).astype(jnp.bfloat16)
    return (d_out_b, d_gate_b, d_cross_b)


def front_backward(
    pair_rows, projected, pair_mask, d_left, d_right, d_gate_b, w_proj, w_gate, d_up
):
    hidden_width = w_proj.shape[1] // 4
    left_gate = jax.nn.sigmoid(projected[:, :hidden_width])
    left_value = projected[:, hidden_width : 2 * hidden_width]
    right_gate = jax.nn.sigmoid(projected[:, 2 * hidden_width : 3 * hidden_width])
    right_value = projected[:, 3 * hidden_width :]
    d_proj = jnp.concatenate(
        [
            d_left * left_value * pair_mask * left_gate * (1.0 - left_gate),
            d_left * left_gate * pair_mask,
            d_right * right_value * pair_mask * right_gate * (1.0 - right_gate),
            d_right * right_gate * pair_mask,
        ],
        axis=1,
    ).astype(jnp.bfloat16)
    d_normed = jnp.dot(d_proj, w_proj.T, preferred_element_type=jnp.float32) + jnp.dot(
        d_gate_b, w_gate.T, preferred_element_type=jnp.float32
    )
    d_pair = (d_up + norm_back(pair_rows, d_normed)).astype(jnp.bfloat16)
    return (d_proj, d_pair)


def to_channels(stacked, row_block, col_block):
    groups = stacked.shape[0]
    col_groups = lax.axis_size(("sub", "pair"))
    sectioning = stacked[None]
    arrived = lax.all_to_all(sectioning, ("sub", "pair"), split_axis=2, concat_axis=0, tiled=True)
    channel_share = arrived.shape[2]
    arrived = arrived.reshape(col_groups, groups, channel_share, row_block, col_block)
    return arrived.transpose(1, 2, 3, 0, 4).reshape(
        groups, channel_share, row_block, col_groups * col_block
    )


def from_channels(stacked, row_block, col_block):
    groups = stacked.shape[0]
    arrived = lax.all_to_all(stacked, ("sub", "pair"), split_axis=3, concat_axis=1, tiled=True)
    return arrived.transpose(0, 2, 3, 1).reshape(groups, row_block * col_block, arrived.shape[1])


def on_device(pair_act, residue_mask, w_proj, w_gate, w_out, d_transposed):
    row_block, col_block, channels = pair_act.shape
    row_count = lax.axis_size("row")
    col_groups = lax.axis_size(("sub", "pair"))
    crop_length = row_block * row_count
    block_width = col_block // row_count
    group_width = row_count // col_groups
    local_rows = row_block * col_block
    row_start = lax.axis_index("row") * row_block
    col_start = lax.axis_index(("sub", "pair")) * col_block
    row_valid = lax.dynamic_slice_in_dim(residue_mask, row_start, row_block, 0).astype(jnp.float32)
    col_valid = lax.dynamic_slice_in_dim(residue_mask, col_start, col_block, 0).astype(jnp.float32)
    pair_mask = (row_valid[:, None] * col_valid[None, :]).reshape(local_rows, 1)
    pair_rows = pair_act.reshape(local_rows, channels).astype(jnp.float32)
    normed, projected, left_b, right_b, gate_act = front_forward(
        pair_rows, w_proj, w_gate, pair_mask
    )
    paired = to_channels(jnp.stack([left_b.T, right_b.T]), row_block, col_block)
    left_t = paired[0]
    right_t = paired[1]
    crossed = jnp.einsum(
        "cik,cjk->cij",
        left_t,
        lax.all_gather(right_t, "row", axis=1, tiled=True),
        preferred_element_type=jnp.float32,
    )
    crossed_rows = from_channels(crossed.astype(jnp.bfloat16)[None], row_block, col_block)[0]
    normed_x, out_proj, updated = back_forward(crossed_rows, gate_act, pair_rows, w_out)
    updated_b = updated.astype(jnp.bfloat16).reshape(
        row_block, group_width, col_groups, block_width, channels
    )
    spread_cols = lax.all_to_all(
        updated_b, ("sub", "pair"), split_axis=2, concat_axis=2, tiled=True
    )
    regrouped = spread_cols.transpose(2, 1, 0, 3, 4).reshape(
        row_count, row_block, block_width, channels
    )
    turned = lax.all_to_all(regrouped, "row", split_axis=0, concat_axis=1, tiled=True)
    transposed = turned.reshape(crop_length, block_width, channels).transpose(1, 0, 2)
    back_in = d_transposed.transpose(1, 0, 2).reshape(row_count, row_block, block_width, channels)
    returned = lax.all_to_all(back_in, "row", split_axis=0, concat_axis=0, tiled=True)
    regrouped_back = returned.reshape(
        col_groups, group_width, row_block, block_width, channels
    ).transpose(2, 1, 0, 3, 4)
    restored = lax.all_to_all(
        regrouped_back, ("sub", "pair"), split_axis=2, concat_axis=2, tiled=True
    )
    d_up = restored.reshape(local_rows, channels).astype(jnp.float32)
    d_out_b, d_gate_b, d_cross_b = back_backward(crossed_rows, out_proj, gate_act, w_out, d_up)
    d_cross_t = to_channels(d_cross_b.T[None], row_block, col_block)[0]
    d_cross_cols = lax.all_to_all(d_cross_t, "row", split_axis=2, concat_axis=1, tiled=True)
    left_part = jnp.einsum(
        "cij,cjk->cik",
        d_cross_t,
        lax.all_gather(right_t, "row", axis=1, tiled=True),
        preferred_element_type=jnp.float32,
    )
    right_part = jnp.einsum(
        "cij,cik->cjk",
        d_cross_cols,
        lax.all_gather(left_t, "row", axis=1, tiled=True),
        preferred_element_type=jnp.float32,
    )
    d_rows_back = from_channels(
        jnp.stack([left_part, right_part]).astype(jnp.bfloat16), row_block, col_block
    )
    d_proj, d_pair = front_backward(
        pair_rows,
        projected,
        pair_mask,
        d_rows_back[0].astype(jnp.float32),
        d_rows_back[1].astype(jnp.float32),
        d_gate_b,
        w_proj,
        w_gate,
        d_up,
    )
    weight_terms = (
        jnp.einsum("rc,rd->cd", normed, d_proj, preferred_element_type=jnp.float32),
        jnp.einsum("rc,rd->cd", normed, d_gate_b, preferred_element_type=jnp.float32),
        jnp.einsum("rc,rd->cd", normed_x, d_out_b, preferred_element_type=jnp.float32),
    )
    g_proj, g_gate, g_out = lax.psum(
        (weight_terms[0], weight_terms[1], weight_terms[2]), ("row", "sub", "pair")
    )
    return (
        transposed,
        d_pair.reshape(row_block, col_block, channels),
        g_proj / crop_length,
        g_gate / crop_length,
        g_out / crop_length,
    )


MESH = pl.DeviceIdType.MESH
F32 = jnp.float32
BF16 = jnp.bfloat16


def norm_rows(values):
    row_mean = jnp.mean(values, axis=-1, keepdims=True)
    centred = values - row_mean
    row_var = jnp.mean(centred * centred, axis=-1, keepdims=True)
    scale = lax.rsqrt(row_var + epsilon)
    return centred * scale, scale


def norm_rows_back(unit, scale, cotangent):
    first = jnp.mean(cotangent, axis=-1, keepdims=True)
    second = jnp.mean(cotangent * unit, axis=-1, keepdims=True)
    return scale * (cotangent - first - unit * second)


def sigmoid(values):
    return 0.5 * jnp.tanh(0.5 * values) + 0.5


def dot_nn(a, b):
    return lax.dot_general(a, b, (((1,), (0,)), ((), ())), preferred_element_type=F32)


def dot_nt(a, b):
    return lax.dot_general(a, b, (((1,), (1,)), ((), ())), preferred_element_type=F32)


def dot_tn(a, b):
    return lax.dot_general(a, b, (((0,), (0,)), ((), ())), preferred_element_type=F32)


def triangle(out, entry, table, length, block=8):
    def step(at, carry):
        totals = [None] * block
        for s in range(length):
            rows = table[s]
            for q in range(block):
                term = entry(at * block + q, s) * rows
                totals[q] = term if s == 0 else totals[q] + term
        for q in range(block):
            out[at * block + q] = totals[q]
        return carry

    lax.fori_loop(0, length // block, step, 0)


def get(ref, at, sizes, shape):
    row_block, col_block, width = shape
    return jnp.concatenate(
        [
            ref[pl.ds(at * row_block, row_block), g * col_block : (g + 1) * col_block].reshape(
                row_block * col_block, width
            )
            for g in range(sizes[1] * sizes[2])
        ],
        axis=0,
    )


def put(ref, at, sizes, shape, values):
    row_block, col_block, width = shape
    half = row_block * col_block
    for g in range(sizes[1] * sizes[2]):
        ref[pl.ds(at * row_block, row_block), g * col_block : (g + 1) * col_block] = values[
            g * half : (g + 1) * half
        ].reshape(row_block, col_block, width)


def front_kernel(
    sizes, shape,
    pair_hbm, cot_hbm, mask_hbm, w_proj_hbm, w_gate_hbm,
    cot_all, pair, gate, left, right, crossed, l_one, l_two, r_one, r_two, normed,
    pair_all, right_by_k, w_proj, w_gate, mask_row, mask, own_sem, send_sem, recv_sem,
):
    rows, subs, pairs = sizes
    row_block, col_block, width = shape
    col_groups = subs * pairs
    length = rows * row_block
    half = row_block * col_block
    band = row_block * length
    r, x, c = lax.axis_index("row"), lax.axis_index("sub"), lax.axis_index("pair")

    def slot(row, sub, pair_at):
        return (row * subs + sub) * pairs + pair_at

    me = slot(r, x, c)
    if rows == 4:
        order = [r, r + 1 - 2 * (r % 2), r + 2 - 4 * (r // 2), 3 - r]
    else:
        order = [(r + step) % rows for step in range(rows)]
    far_first = [(order[q], sub) for q in reversed(range(1, rows)) for sub in (1 - x, x)] + [(r, 1 - x)]

    local = [
        pltpu.make_async_copy(pair_hbm, pair_all.at[me], own_sem.at[0]),
        pltpu.make_async_copy(cot_hbm, cot_all.at[me], own_sem.at[1]),
        pltpu.make_async_copy(mask_hbm, mask_row, own_sem.at[2]),
        pltpu.make_async_copy(w_proj_hbm, w_proj, own_sem.at[3]),
        pltpu.make_async_copy(w_gate_hbm, w_gate, own_sem.at[4]),
    ]
    for one in local:
        one.start()

    barrier = pltpu.get_barrier_semaphore()
    for row, sub in far_first:
        pl.semaphore_signal(barrier, inc=1, device_id={"row": row, "sub": sub}, device_id_type=MESH)
    pl.semaphore_signal(barrier, inc=1, device_id={"pair": 1 - c}, device_id_type=MESH)

    local[2].wait()
    place = lax.broadcasted_iota(jnp.int32, (length, width), 0)
    col_mask = jnp.zeros((length, width), F32)
    for i in range(length):
        col_mask = jnp.where(place == i, mask_row[i].astype(F32), col_mask)
    for i in range(length):
        mask[i] = col_mask * mask_row[i].astype(F32)
    for one in (local[0], local[1], local[3], local[4]):
        one.wait()
    pl.semaphore_wait(barrier, len(far_first) + 1)

    buffers = (pair_all, cot_all)
    sent = ([], [])

    def copy(kind, owner, number, target):
        return pltpu.make_async_remote_copy(
            src_ref=buffers[kind].at[owner],
            dst_ref=buffers[kind].at[owner],
            send_sem=send_sem.at[kind, number],
            recv_sem=recv_sem.at[kind, owner],
            device_id=target,
            device_id_type=MESH,
        )

    def send(kind, owner, target):
        one = copy(kind, owner, len(sent[kind]), target)
        one.start()
        sent[kind].append(one)

    other = {"pair": 1 - c}

    def send_own(kind):
        for row, sub in far_first:
            send(kind, me, {"row": row, "sub": sub})
        send(kind, me, other)

    def pass_on(kind, q):
        for sub in (1 - x,) if q == 0 else (x, 1 - x):
            owner = slot(order[q], sub, c)
            copy(kind, owner, 0, other).wait_recv()
            send(kind, owner, other)

    def from_other(kind, q):
        for sub in (x, 1 - x):
            copy(kind, slot(order[q], sub, 1 - c), 0, other).wait_recv()

    def front(q):
        at = order[q]
        rows_at = pl.ds(pl.multiple_of(at * band, band), band)
        values = pair_all[pl.ds(at * col_groups, col_groups)].reshape(band, width).astype(F32)
        put(pair, at, sizes, shape, values)
        unit, _ = norm_rows(values)
        unit_b = unit.astype(BF16)
        normed[rows_at] = unit_b
        m = get(mask, at, sizes, shape)
        put(gate, at, sizes, shape, sigmoid(dot_nn(unit_b, w_gate[...])))
        projected = dot_nn(unit_b, w_proj[...])
        for base, ref, one, two in ((0, left, l_one, l_two), (2, right, r_one, r_two)):
            s = sigmoid(projected[:, base * width : (base + 1) * width])
            v = projected[:, (base + 1) * width : (base + 2) * width]
            sm = s * m
            vs = v * sm
            one[rows_at] = sm
            two[rows_at] = vs * (1.0 - s)
            put(ref, at, sizes, shape, vs.astype(BF16).astype(F32))

    right_flat = right.reshape(length * length, width)

    def tile(q):
        return pl.ds(pl.multiple_of(order[q] * row_block, row_block), row_block)

    def cross_part(q, targets, block):
        def step(at, carry):
            first = order[q] * row_block + at * block
            totals = [[None] * len(targets) for _ in range(block)]
            for s in range(length):
                tables = [right_by_k[s, tile(t)] for t in targets]
                for b in range(block):
                    entry = left[first + b, pl.ds(s, 1)]
                    for n, table in enumerate(tables):
                        term = entry * table
                        totals[b][n] = term if s == 0 else totals[b][n] + term
            for b in range(block):
                for n, t in enumerate(targets):
                    crossed[first + b, tile(t)] = totals[b][n]
            return carry

        lax.fori_loop(0, row_block // block, step, 0)

    def cross(q):
        start = order[q] * row_block * length
        for k in range(length):
            right_by_k[k, tile(q)] = right_flat[pl.ds(start + k, row_block, stride=length)]
        cross_part(q, list(range(q + 1)), 8 if q < 2 else 4)
        for earlier in range(q):
            cross_part(earlier, [q], 8)

    send_own(0)
    send_own(1)
    pass_on(0, 0)
    pass_on(0, 1)
    from_other(0, 0)
    front(0)
    for q in range(2, rows):
        pass_on(0, q)
    cross(0)
    for q in range(1, rows):
        from_other(0, q)
        front(q)
        cross(q)
        if q == rows - 2:
            pass_on(1, 0)
    for q in range(1, rows):
        pass_on(1, q)
    for q in range(rows):
        from_other(1, q)
    for kind in (0, 1):
        for one in sent[kind]:
            one.wait_send()


def crop_kernel(
    sizes, shape,
    cot_all, pair, gate, left, right, crossed, l_one, l_two, r_one, r_two, normed,
    w_proj_ref, w_gate_ref, w_out_ref,
    turned_ref, d_pair_ref, g_proj_ref, g_gate_ref, g_out_ref,
    cot_flat, d_up,
    d_cross, d_left, d_right, d_gate, up_flat, d_proj, d_gate_b,
):
    rows, subs, pairs = sizes
    row_block, col_block, width = shape
    col_groups = subs * pairs
    length = rows * row_block
    half = row_block * col_block
    band = row_block * length
    r = lax.axis_index("row")
    cg = lax.axis_index("sub") * pairs + lax.axis_index("pair")

    cot_flat[...] = cot_all[...].reshape(length * length, width).astype(F32)
    for i in range(length):
        d_up[i] = cot_flat[pl.ds(i, length, stride=length)]

    g_out_ref[...] = jnp.zeros_like(g_out_ref)
    g_proj_ref[...] = jnp.zeros_like(g_proj_ref)
    g_gate_ref[...] = jnp.zeros_like(g_gate_ref)

    def middle(at, carry):
        here = pl.ds(at * row_block, row_block)

        def flat(ref):
            return ref[here].reshape(band, width)

        unit, scale = norm_rows(flat(crossed).astype(BF16).astype(F32))
        unit_b = unit.astype(BF16)
        w_out = w_out_ref[...]
        out_proj = dot_nn(unit_b, w_out)
        g = flat(gate)
        up = flat(d_up)
        gated = g * out_proj
        up_flat[pl.ds(pl.multiple_of(at * band, band), band)] = flat(pair) + gated
        d_out_b = (g * up).astype(BF16)
        d_gate[here] = (gated * up * (1.0 - g)).reshape(row_block, length, width)
        d_unit = dot_nt(d_out_b, w_out)
        back = norm_rows_back(unit, scale, d_unit)
        d_cross[here] = back.astype(BF16).astype(F32).reshape(row_block, length, width)
        g_out_ref[...] += dot_tn(unit_b, d_out_b)
        return carry

    lax.fori_loop(0, rows, middle, 0, unroll=True)

    triangle(d_left, lambda a, s: d_cross[a, pl.ds(s, 1)], right, length)
    triangle(d_right, lambda a, s: d_cross[s, pl.ds(a, 1)], left, length)

    def finish(at, carry):
        rows_at = pl.ds(pl.multiple_of(at * band, band), band)
        dl, dr = get(d_left, at, sizes, shape), get(d_right, at, sizes, shape)
        parts = (dl * l_two[rows_at], dl * l_one[rows_at], dr * r_two[rows_at], dr * r_one[rows_at])
        unit_b = normed[rows_at]
        for q, part in enumerate(parts):
            part_b = part.astype(BF16)
            d_proj[rows_at, q * width : (q + 1) * width] = part_b
        g_proj_ref[...] += dot_tn(unit_b, d_proj[rows_at])
        gate_b = get(d_gate, at, sizes, shape).astype(BF16)
        d_gate_b[rows_at] = gate_b
        g_gate_ref[...] += dot_tn(unit_b, gate_b)
        return carry

    lax.fori_loop(0, rows, finish, 0, unroll=True)

    share = 1.0 / length
    g_proj_ref[...] = g_proj_ref[...] * share
    g_gate_ref[...] = g_gate_ref[...] * share
    g_out_ref[...] = g_out_ref[...] * share

    own = r * col_groups + cg
    own_rows = pl.ds(pl.multiple_of(own * half, half), half)
    d_normed = dot_nt(d_proj[own_rows], w_proj_ref[...]) + dot_nt(d_gate_b[own_rows], w_gate_ref[...])

    def own_block(ref):
        columns = pl.ds(pl.multiple_of(cg * col_block, col_block), col_block)
        return ref[pl.ds(r * row_block, row_block), columns].reshape(half, width)

    unit, scale = norm_rows(own_block(pair))
    up = own_block(d_up)
    d_pair_ref[...] = (up + norm_rows_back(unit, scale, d_normed)).astype(BF16)

    turned_rows = half // length
    for q in range(turned_rows):
        turned_ref[q * length : (q + 1) * length] = up_flat[
            pl.ds(own * turned_rows + q, length, stride=length)
        ].astype(BF16)


def on_device_whole(sizes, pair_act, residue_mask, w_proj, w_gate, w_out, d_transposed):
    row_block, col_block, channels = pair_act.shape
    rows, subs, pairs = sizes
    devices = rows * subs * pairs
    length = rows * row_block
    half = row_block * col_block
    pair_own = pair_act.reshape(half, channels)
    cot_own = d_transposed.reshape(half, channels)
    shape = (row_block, col_block, channels)
    in_vmem = pl.BlockSpec(memory_space=pltpu.VMEM)
    in_hbm = pl.BlockSpec(memory_space=pltpu.HBM)
    cube = (length, length, channels)
    flat = (length * length, channels)
    kept = [jax.ShapeDtypeStruct(cube, F32)] * 5 + [jax.ShapeDtypeStruct(flat, F32)] * 4
    held = pl.pallas_call(
        functools.partial(front_kernel, sizes, shape),
        out_shape=[
            jax.ShapeDtypeStruct((devices, half, channels), BF16),
            *kept,
            jax.ShapeDtypeStruct(flat, BF16),
        ],
        in_specs=[in_hbm] * 5,
        out_specs=[in_vmem] * 11,
        scratch_shapes=[
            pltpu.VMEM((devices, half, channels), BF16),
            pltpu.VMEM(cube, F32),
            pltpu.VMEM(w_proj.shape, BF16),
            pltpu.VMEM(w_gate.shape, BF16),
            pltpu.SMEM((length,), jnp.int32),
            pltpu.VMEM(cube, F32),
            pltpu.SemaphoreType.DMA((5,)),
            pltpu.SemaphoreType.DMA((2, devices)),
            pltpu.SemaphoreType.DMA((2, devices)),
        ],
        compiler_params=pltpu.CompilerParams(
            collective_id=0, has_side_effects=True, vmem_limit_bytes=16 * 1024 * 1024
        ),
        name="front",
    )(*(pltpu.with_memory_space_constraint(each, pltpu.HBM) for each in (pair_own, cot_own, residue_mask, w_proj, w_gate)))
    cube_room = pltpu.VMEM(cube, F32)
    flat_room = pltpu.VMEM(flat, F32)
    turned, d_pair, g_proj, g_gate, g_out = pl.pallas_call(
        functools.partial(crop_kernel, sizes, shape),
        out_shape=(
            jax.ShapeDtypeStruct((half, channels), BF16),
            jax.ShapeDtypeStruct((half, channels), BF16),
            jax.ShapeDtypeStruct(w_proj.shape, F32),
            jax.ShapeDtypeStruct(w_gate.shape, F32),
            jax.ShapeDtypeStruct(w_out.shape, F32),
        ),
        in_specs=[in_vmem] * 14,
        out_specs=[in_vmem] * 5,
        scratch_shapes=[
            flat_room, cube_room,
            cube_room, cube_room, cube_room, cube_room, flat_room,
            pltpu.VMEM((length * length, w_proj.shape[1]), BF16),
            pltpu.VMEM(flat, BF16),
        ],
        compiler_params=pltpu.CompilerParams(vmem_limit_bytes=24 * 1024 * 1024),
        name="crop",
    )(*held, w_proj, w_gate, w_out)
    return (
        turned.reshape(d_transposed.shape),
        d_pair.reshape(pair_act.shape),
        g_proj,
        g_gate,
        g_out,
    )


def choose(sizes, pair_act, residue_mask, w_proj, w_gate, w_out, d_transposed):
    row_block, col_block, channels = pair_act.shape
    length = sizes[0] * row_block
    fits = (
        length <= 32
        and row_block % 8 == 0
        and col_block % 8 == 0
        and sizes[1:] == (2, 2)
        and w_out.shape == (128, 128)
        and w_proj.shape == (128, 512)
    )
    body = functools.partial(on_device_whole, sizes) if fits else on_device
    return body(pair_act, residue_mask, w_proj, w_gate, w_out, d_transposed)


def solution(mesh):
    in_specs = (
        P(("crops", "row"), ("sub", "pair"), None),
        P("crops"),
        P(),
        P(),
        P(),
        P(("crops", "row", "sub", "pair"), None, None),
    )
    out_specs = (
        P(("crops", "row", "sub", "pair"), None, None),
        P(("crops", "row"), ("sub", "pair"), None),
        P("crops", None),
        P("crops", None),
        P("crops", None),
    )
    sizes = (mesh.shape["row"], mesh.shape["sub"], mesh.shape["pair"])
    return jax.shard_map(
        functools.partial(choose, sizes), mesh=mesh, in_specs=in_specs, out_specs=out_specs, check_vma=False
    )
```

```python
import functools

import jax
import jax.numpy as jnp
from jax import lax
from jax.experimental import pallas as pl
from jax.experimental.pallas import tpu as pltpu
from jax.sharding import PartitionSpec as P

epsilon = 1e-05


def layer_norm(values):
    row_mean = jnp.mean(values, axis=-1, keepdims=True)
    centred = values - row_mean
    row_var = jnp.mean(centred * centred, axis=-1, keepdims=True)
    return centred * lax.rsqrt(row_var + epsilon)


def norm_back(values, cotangent):
    return jax.vjp(layer_norm, values)[1](cotangent)[0]


def front_forward(pair_rows, w_proj, w_gate, pair_mask):
    hidden_width = w_proj.shape[1] // 4
    normed = layer_norm(pair_rows).astype(jnp.bfloat16)
    projected = jnp.dot(normed, w_proj, preferred_element_type=jnp.float32)
    gate_pre = jnp.dot(normed, w_gate, preferred_element_type=jnp.float32)
    left_b = (
        jax.nn.sigmoid(projected[:, :hidden_width])
        * projected[:, hidden_width : 2 * hidden_width]
        * pair_mask
    )
    right_b = (
        jax.nn.sigmoid(projected[:, 2 * hidden_width : 3 * hidden_width])
        * projected[:, 3 * hidden_width :]
        * pair_mask
    )
    return (
        normed,
        projected,
        left_b.astype(jnp.bfloat16),
        right_b.astype(jnp.bfloat16),
        jax.nn.sigmoid(gate_pre),
    )


def back_forward(crossed_rows, gate_act, pair_rows, w_out):
    normed_x = layer_norm(crossed_rows.astype(jnp.float32)).astype(jnp.bfloat16)
    out_proj = jnp.dot(normed_x, w_out, preferred_element_type=jnp.float32)
    return (normed_x, out_proj, pair_rows + gate_act * out_proj)


def back_backward(crossed_rows, out_proj, gate_act, w_out, d_up):
    d_out_b = (gate_act * d_up).astype(jnp.bfloat16)
    d_gate_b = (out_proj * d_up * gate_act * (1.0 - gate_act)).astype(jnp.bfloat16)
    d_normed_x = jnp.dot(d_out_b, w_out.T, preferred_element_type=jnp.float32)
    d_cross_b = norm_back(crossed_rows.astype(jnp.float32), d_normed_x).astype(jnp.bfloat16)
    return (d_out_b, d_gate_b, d_cross_b)


def front_backward(
    pair_rows, projected, pair_mask, d_left, d_right, d_gate_b, w_proj, w_gate, d_up
):
    hidden_width = w_proj.shape[1] // 4
    left_gate = jax.nn.sigmoid(projected[:, :hidden_width])
    left_value = projected[:, hidden_width : 2 * hidden_width]
    right_gate = jax.nn.sigmoid(projected[:, 2 * hidden_width : 3 * hidden_width])
    right_value = projected[:, 3 * hidden_width :]
    d_proj = jnp.concatenate(
        [
            d_left * left_value * pair_mask * left_gate * (1.0 - left_gate),
            d_left * left_gate * pair_mask,
            d_right * right_value * pair_mask * right_gate * (1.0 - right_gate),
            d_right * right_gate * pair_mask,
        ],
        axis=1,
    ).astype(jnp.bfloat16)
    d_normed = jnp.dot(d_proj, w_proj.T, preferred_element_type=jnp.float32) + jnp.dot(
        d_gate_b, w_gate.T, preferred_element_type=jnp.float32
    )
    d_pair = (d_up + norm_back(pair_rows, d_normed)).astype(jnp.bfloat16)
    return (d_proj, d_pair)


def to_channels(stacked, row_block, col_block):
    groups = stacked.shape[0]
    col_groups = lax.axis_size(("sub", "pair"))
    sectioning = stacked[None]
    arrived = lax.all_to_all(sectioning, ("sub", "pair"), split_axis=2, concat_axis=0, tiled=True)
    channel_share = arrived.shape[2]
    arrived = arrived.reshape(col_groups, groups, channel_share, row_block, col_block)
    return arrived.transpose(1, 2, 3, 0, 4).reshape(
        groups, channel_share, row_block, col_groups * col_block
    )


def from_channels(stacked, row_block, col_block):
    groups = stacked.shape[0]
    arrived = lax.all_to_all(stacked, ("sub", "pair"), split_axis=3, concat_axis=1, tiled=True)
    return arrived.transpose(0, 2, 3, 1).reshape(groups, row_block * col_block, arrived.shape[1])


def on_device(pair_act, residue_mask, w_proj, w_gate, w_out, d_transposed):
    row_block, col_block, channels = pair_act.shape
    row_count = lax.axis_size("row")
    col_groups = lax.axis_size(("sub", "pair"))
    crop_length = row_block * row_count
    block_width = col_block // row_count
    group_width = row_count // col_groups
    local_rows = row_block * col_block
    row_start = lax.axis_index("row") * row_block
    col_start = lax.axis_index(("sub", "pair")) * col_block
    row_valid = lax.dynamic_slice_in_dim(residue_mask, row_start, row_block, 0).astype(jnp.float32)
    col_valid = lax.dynamic_slice_in_dim(residue_mask, col_start, col_block, 0).astype(jnp.float32)
    pair_mask = (row_valid[:, None] * col_valid[None, :]).reshape(local_rows, 1)
    pair_rows = pair_act.reshape(local_rows, channels).astype(jnp.float32)
    normed, projected, left_b, right_b, gate_act = front_forward(
        pair_rows, w_proj, w_gate, pair_mask
    )
    paired = to_channels(jnp.stack([left_b.T, right_b.T]), row_block, col_block)
    left_t = paired[0]
    right_t = paired[1]
    crossed = jnp.einsum(
        "cik,cjk->cij",
        left_t,
        lax.all_gather(right_t, "row", axis=1, tiled=True),
        preferred_element_type=jnp.float32,
    )
    crossed_rows = from_channels(crossed.astype(jnp.bfloat16)[None], row_block, col_block)[0]
    normed_x, out_proj, updated = back_forward(crossed_rows, gate_act, pair_rows, w_out)
    updated_b = updated.astype(jnp.bfloat16).reshape(
        row_block, group_width, col_groups, block_width, channels
    )
    spread_cols = lax.all_to_all(
        updated_b, ("sub", "pair"), split_axis=2, concat_axis=2, tiled=True
    )
    regrouped = spread_cols.transpose(2, 1, 0, 3, 4).reshape(
        row_count, row_block, block_width, channels
    )
    turned = lax.all_to_all(regrouped, "row", split_axis=0, concat_axis=1, tiled=True)
    transposed = turned.reshape(crop_length, block_width, channels).transpose(1, 0, 2)
    back_in = d_transposed.transpose(1, 0, 2).reshape(row_count, row_block, block_width, channels)
    returned = lax.all_to_all(back_in, "row", split_axis=0, concat_axis=0, tiled=True)
    regrouped_back = returned.reshape(
        col_groups, group_width, row_block, block_width, channels
    ).transpose(2, 1, 0, 3, 4)
    restored = lax.all_to_all(
        regrouped_back, ("sub", "pair"), split_axis=2, concat_axis=2, tiled=True
    )
    d_up = restored.reshape(local_rows, channels).astype(jnp.float32)
    d_out_b, d_gate_b, d_cross_b = back_backward(crossed_rows, out_proj, gate_act, w_out, d_up)
    d_cross_t = to_channels(d_cross_b.T[None], row_block, col_block)[0]
    d_cross_cols = lax.all_to_all(d_cross_t, "row", split_axis=2, concat_axis=1, tiled=True)
    left_part = jnp.einsum(
        "cij,cjk->cik",
        d_cross_t,
        lax.all_gather(right_t, "row", axis=1, tiled=True),
        preferred_element_type=jnp.float32,
    )
    right_part = jnp.einsum(
        "cij,cik->cjk",
        d_cross_cols,
        lax.all_gather(left_t, "row", axis=1, tiled=True),
        preferred_element_type=jnp.float32,
    )
    d_rows_back = from_channels(
        jnp.stack([left_part, right_part]).astype(jnp.bfloat16), row_block, col_block
    )
    d_proj, d_pair = front_backward(
        pair_rows,
        projected,
        pair_mask,
        d_rows_back[0].astype(jnp.float32),
        d_rows_back[1].astype(jnp.float32),
        d_gate_b,
        w_proj,
        w_gate,
        d_up,
    )
    weight_terms = (
        jnp.einsum("rc,rd->cd", normed, d_proj, preferred_element_type=jnp.float32),
        jnp.einsum("rc,rd->cd", normed, d_gate_b, preferred_element_type=jnp.float32),
        jnp.einsum("rc,rd->cd", normed_x, d_out_b, preferred_element_type=jnp.float32),
    )
    g_proj, g_gate, g_out = lax.psum(
        (weight_terms[0], weight_terms[1], weight_terms[2]), ("row", "sub", "pair")
    )
    return (
        transposed,
        d_pair.reshape(row_block, col_block, channels),
        g_proj / crop_length,
        g_gate / crop_length,
        g_out / crop_length,
    )


MESH = pl.DeviceIdType.MESH
F32 = jnp.float32
BF16 = jnp.bfloat16


def norm_rows(values):
    row_mean = jnp.mean(values, axis=-1, keepdims=True)
    centred = values - row_mean
    row_var = jnp.mean(centred * centred, axis=-1, keepdims=True)
    scale = lax.rsqrt(row_var + epsilon)
    return centred * scale, scale


def norm_rows_back(unit, scale, cotangent):
    first = jnp.mean(cotangent, axis=-1, keepdims=True)
    second = jnp.mean(cotangent * unit, axis=-1, keepdims=True)
    return scale * (cotangent - first - unit * second)


def sigmoid(values):
    return 0.5 * jnp.tanh(0.5 * values) + 0.5


def dot_nn(a, b):
    return lax.dot_general(a, b, (((1,), (0,)), ((), ())), preferred_element_type=F32)


def dot_nt(a, b):
    return lax.dot_general(a, b, (((1,), (1,)), ((), ())), preferred_element_type=F32)


def dot_tn(a, b):
    return lax.dot_general(a, b, (((0,), (0,)), ((), ())), preferred_element_type=F32)


def triangle(out, entry, table, length, block=8):
    def step(at, carry):
        totals = [None] * block
        for s in range(length):
            rows = table[s]
            for q in range(block):
                term = entry(at * block + q, s) * rows
                totals[q] = term if s == 0 else totals[q] + term
        for q in range(block):
            out[at * block + q] = totals[q]
        return carry

    lax.fori_loop(0, length // block, step, 0)


def get(ref, at, sizes, shape):
    row_block, col_block, width = shape
    return jnp.concatenate(
        [
            ref[pl.ds(at * row_block, row_block), g * col_block : (g + 1) * col_block].reshape(
                row_block * col_block, width
            )
            for g in range(sizes[1] * sizes[2])
        ],
        axis=0,
    )


def put(ref, at, sizes, shape, values):
    row_block, col_block, width = shape
    half = row_block * col_block
    for g in range(sizes[1] * sizes[2]):
        ref[pl.ds(at * row_block, row_block), g * col_block : (g + 1) * col_block] = values[
            g * half : (g + 1) * half
        ].reshape(row_block, col_block, width)


def front_kernel(
    sizes, shape,
    pair_hbm, cot_hbm, mask_hbm, w_proj_hbm, w_gate_hbm, w_out_hbm,
    cot_all, pair, gate, left, right, unit_x, scale_x, gated, l_one, l_two, r_one, r_two, normed,
    pair_all, right_by_k, crossed, w_proj, w_gate, w_out, mask_row, mask, own_sem, send_sem, recv_sem,
):
    rows, subs, pairs = sizes
    row_block, col_block, width = shape
    col_groups = subs * pairs
    length = rows * row_block
    half = row_block * col_block
    band = row_block * length
    r, x, c = lax.axis_index("row"), lax.axis_index("sub"), lax.axis_index("pair")

    def slot(row, sub, pair_at):
        return (row * subs + sub) * pairs + pair_at

    me = slot(r, x, c)
    if rows == 4:
        order = [r, r + 1 - 2 * (r % 2), r + 2 - 4 * (r // 2), 3 - r]
    else:
        order = [(r + step) % rows for step in range(rows)]
    far_first = [(order[q], sub) for q in reversed(range(1, rows)) for sub in (1 - x, x)] + [(r, 1 - x)]

    local = [
        pltpu.make_async_copy(pair_hbm, pair_all.at[me], own_sem.at[0]),
        pltpu.make_async_copy(cot_hbm, cot_all.at[me], own_sem.at[1]),
        pltpu.make_async_copy(mask_hbm, mask_row, own_sem.at[2]),
        pltpu.make_async_copy(w_proj_hbm, w_proj, own_sem.at[3]),
        pltpu.make_async_copy(w_gate_hbm, w_gate, own_sem.at[4]),
        pltpu.make_async_copy(w_out_hbm, w_out, own_sem.at[5]),
    ]
    for one in local:
        one.start()

    barrier = pltpu.get_barrier_semaphore()
    for row, sub in far_first:
        pl.semaphore_signal(barrier, inc=1, device_id={"row": row, "sub": sub}, device_id_type=MESH)
    pl.semaphore_signal(barrier, inc=1, device_id={"pair": 1 - c}, device_id_type=MESH)

    local[2].wait()
    place = lax.broadcasted_iota(jnp.int32, (length, width), 0)
    col_mask = jnp.zeros((length, width), F32)
    for i in range(length):
        col_mask = jnp.where(place == i, mask_row[i].astype(F32), col_mask)
    for i in range(length):
        mask[i] = col_mask * mask_row[i].astype(F32)
    for one in local[:2] + local[3:]:
        one.wait()
    pl.semaphore_wait(barrier, len(far_first) + 1)

    buffers = (pair_all, cot_all)
    sent = ([], [])

    def copy(kind, owner, number, target):
        return pltpu.make_async_remote_copy(
            src_ref=buffers[kind].at[owner],
            dst_ref=buffers[kind].at[owner],
            send_sem=send_sem.at[kind, number],
            recv_sem=recv_sem.at[kind, owner],
            device_id=target,
            device_id_type=MESH,
        )

    def send(kind, owner, target):
        one = copy(kind, owner, len(sent[kind]), target)
        one.start()
        sent[kind].append(one)

    other = {"pair": 1 - c}

    def send_own(kind):
        for row, sub in far_first:
            send(kind, me, {"row": row, "sub": sub})
        send(kind, me, other)

    def pass_on(kind, q):
        for sub in (1 - x,) if q == 0 else (x, 1 - x):
            owner = slot(order[q], sub, c)
            copy(kind, owner, 0, other).wait_recv()
            send(kind, owner, other)

    def from_other(kind, q):
        for sub in (x, 1 - x):
            copy(kind, slot(order[q], sub, 1 - c), 0, other).wait_recv()

    def front(chunks):
        blocks = [(order[q], sub * pairs + core) for q, core in chunks for sub in range(subs)]

        def place_of(at, g):
            rows_at = pl.ds(pl.multiple_of((at * col_groups + g) * half, half), half)
            cols = pl.ds(pl.multiple_of(g * col_block, col_block), col_block)
            return rows_at, (pl.ds(pl.multiple_of(at * row_block, row_block), row_block), cols)

        places = [place_of(at, g) for at, g in blocks]

        def put_flat(ref, values):
            for n, (rows_at, _) in enumerate(places):
                ref[rows_at] = values[n * half : (n + 1) * half]

        def put_cube(ref, values):
            for n, (_, where) in enumerate(places):
                ref[where] = values[n * half : (n + 1) * half].reshape(row_block, col_block, width)

        values = jnp.concatenate([pair_all[at * col_groups + g] for at, g in blocks], axis=0).astype(F32)
        put_cube(pair, values)
        unit, _ = norm_rows(values)
        unit_b = unit.astype(BF16)
        put_flat(normed, unit_b)
        m = jnp.concatenate([mask[where].reshape(half, width) for _, where in places], axis=0)
        put_cube(gate, sigmoid(dot_nn(unit_b, w_gate[...])))
        projected = dot_nn(unit_b, w_proj[...])
        for base, ref, one, two in ((0, left, l_one, l_two), (2, right, r_one, r_two)):
            s = sigmoid(projected[:, base * width : (base + 1) * width])
            v = projected[:, (base + 1) * width : (base + 2) * width]
            sm = s * m
            vs = v * sm
            put_flat(one, sm)
            put_flat(two, vs * (1.0 - s))
            put_cube(ref, vs.astype(BF16).astype(F32))

    right_flat = right.reshape(length * length, width)

    def cross(core, more):
        ks = [(sub * pairs + core) * col_block + at for sub in range(subs) for at in range(col_block)]
        for k in ks:
            right_by_k[k] = right_flat[pl.ds(k, length, stride=length)]

        def step(at, carry):
            totals = [crossed[at * 8 + q] if more else None for q in range(8)]
            for k in ks:
                rows_k = right_by_k[k]
                for q in range(8):
                    term = left[at * 8 + q, pl.ds(k, 1)] * rows_k
                    totals[q] = term if totals[q] is None else totals[q] + term
            for q in range(8):
                crossed[at * 8 + q] = totals[q]
            return carry

        lax.fori_loop(0, length // 8, step, 0)

    send_own(0)
    send_own(1)
    pass_on(0, 0)
    from_other(0, 0)
    front([(0, c), (0, 1 - c)])
    for q in range(1, rows):
        pass_on(0, q)
    front([(q, c) for q in range(1, rows)])
    cross(c, False)
    pass_on(1, 0)
    pass_on(1, 1)
    for q in range(1, rows):
        from_other(0, q)
    front([(q, 1 - c) for q in range(1, rows)])
    for q in range(2, rows):
        pass_on(1, q)
    cross(1 - c, True)

    def second_norm(at, carry):
        here = pl.ds(at * row_block, row_block)
        in_cube = (row_block, length, width)
        held = crossed[here].reshape(band, width).astype(BF16).astype(F32)
        each, scale_rows = norm_rows(held)
        out_proj = dot_nn(each.astype(BF16), w_out[...])
        unit_x[here] = each.reshape(in_cube)
        scale_x[here] = jnp.broadcast_to(scale_rows, each.shape).reshape(in_cube)
        gated[here] = (gate[here].reshape(band, width) * out_proj).reshape(in_cube)
        return carry

    lax.fori_loop(0, rows, second_norm, 0, unroll=True)
    for q in range(rows):
        from_other(1, q)
    for kind in (0, 1):
        for one in sent[kind]:
            one.wait_send()


def crop_kernel(
    sizes, shape,
    cot_all, pair, gate, left, right, unit_x, scale_x, gated, l_one, l_two, r_one, r_two, normed,
    w_proj_ref, w_gate_ref, w_out_ref,
    turned_ref, d_pair_ref, g_proj_ref, g_gate_ref, g_out_ref,
    cot_flat, d_up,
    d_cross, d_left, d_right, d_gate, d_proj, d_gate_b,
):
    rows, subs, pairs = sizes
    row_block, col_block, width = shape
    col_groups = subs * pairs
    length = rows * row_block
    half = row_block * col_block
    band = row_block * length
    r = lax.axis_index("row")
    cg = lax.axis_index("sub") * pairs + lax.axis_index("pair")

    cot_flat[...] = cot_all[...].reshape(length * length, width).astype(F32)
    for i in range(length):
        d_up[i] = cot_flat[pl.ds(i, length, stride=length)]

    g_out_ref[...] = jnp.zeros_like(g_out_ref)
    g_proj_ref[...] = jnp.zeros_like(g_proj_ref)
    g_gate_ref[...] = jnp.zeros_like(g_gate_ref)

    def middle(at, carry):
        here = pl.ds(at * row_block, row_block)

        def flat(ref):
            return ref[here].reshape(band, width)

        unit = flat(unit_x)
        g = flat(gate)
        up = flat(d_up)
        d_out_b = (g * up).astype(BF16)
        d_gate[here] = (flat(gated) * up * (1.0 - g)).reshape(row_block, length, width)
        d_unit = dot_nt(d_out_b, w_out_ref[...])
        back = norm_rows_back(unit, flat(scale_x), d_unit)
        d_cross[here] = back.astype(BF16).astype(F32).reshape(row_block, length, width)
        g_out_ref[...] += dot_tn(unit.astype(BF16), d_out_b)
        return carry

    lax.fori_loop(0, rows, middle, 0, unroll=True)

    triangle(d_left, lambda a, s: d_cross[a, pl.ds(s, 1)], right, length)
    triangle(d_right, lambda a, s: d_cross[s, pl.ds(a, 1)], left, length)

    def finish(at, carry):
        rows_at = pl.ds(pl.multiple_of(at * band, band), band)
        dl, dr = get(d_left, at, sizes, shape), get(d_right, at, sizes, shape)
        parts = (dl * l_two[rows_at], dl * l_one[rows_at], dr * r_two[rows_at], dr * r_one[rows_at])
        unit_b = normed[rows_at]
        for q, part in enumerate(parts):
            part_b = part.astype(BF16)
            d_proj[rows_at, q * width : (q + 1) * width] = part_b
        g_proj_ref[...] += dot_tn(unit_b, d_proj[rows_at])
        gate_b = get(d_gate, at, sizes, shape).astype(BF16)
        d_gate_b[rows_at] = gate_b
        g_gate_ref[...] += dot_tn(unit_b, gate_b)
        return carry

    lax.fori_loop(0, rows, finish, 0, unroll=True)

    share = 1.0 / length
    g_proj_ref[...] = g_proj_ref[...] * share
    g_gate_ref[...] = g_gate_ref[...] * share
    g_out_ref[...] = g_out_ref[...] * share

    own = r * col_groups + cg
    own_rows = pl.ds(pl.multiple_of(own * half, half), half)
    d_normed = dot_nt(d_proj[own_rows], w_proj_ref[...]) + dot_nt(d_gate_b[own_rows], w_gate_ref[...])

    def own_block(ref):
        columns = pl.ds(pl.multiple_of(cg * col_block, col_block), col_block)
        return ref[pl.ds(r * row_block, row_block), columns].reshape(half, width)

    unit, scale = norm_rows(own_block(pair))
    up = own_block(d_up)
    d_pair_ref[...] = (up + norm_rows_back(unit, scale, d_normed)).astype(BF16)

    turned_rows = half // length
    for q in range(turned_rows):
        rows_at = pl.ds(own * turned_rows + q, length, stride=length)
        turned = pair.reshape(length * length, width)[rows_at] + gated.reshape(length * length, width)[rows_at]
        turned_ref[q * length : (q + 1) * length] = turned.astype(BF16)


def on_device_whole(sizes, pair_act, residue_mask, w_proj, w_gate, w_out, d_transposed):
    row_block, col_block, channels = pair_act.shape
    rows, subs, pairs = sizes
    devices = rows * subs * pairs
    length = rows * row_block
    half = row_block * col_block
    pair_own = pair_act.reshape(half, channels)
    cot_own = d_transposed.reshape(half, channels)
    shape = (row_block, col_block, channels)
    in_vmem = pl.BlockSpec(memory_space=pltpu.VMEM)
    in_hbm = pl.BlockSpec(memory_space=pltpu.HBM)
    cube = (length, length, channels)
    flat = (length * length, channels)
    kept = [jax.ShapeDtypeStruct(cube, F32)] * 7 + [jax.ShapeDtypeStruct(flat, F32)] * 4
    held = pl.pallas_call(
        functools.partial(front_kernel, sizes, shape),
        out_shape=[
            jax.ShapeDtypeStruct((devices, half, channels), BF16),
            *kept,
            jax.ShapeDtypeStruct(flat, BF16),
        ],
        in_specs=[in_hbm] * 6,
        out_specs=[in_vmem] * 13,
        scratch_shapes=[
            pltpu.VMEM((devices, half, channels), BF16),
            pltpu.VMEM(cube, F32),
            pltpu.VMEM(cube, F32),
            pltpu.VMEM(w_proj.shape, BF16),
            pltpu.VMEM(w_gate.shape, BF16),
            pltpu.VMEM(w_out.shape, BF16),
            pltpu.SMEM((length,), jnp.int32),
            pltpu.VMEM(cube, F32),
            pltpu.SemaphoreType.DMA((6,)),
            pltpu.SemaphoreType.DMA((2, devices)),
            pltpu.SemaphoreType.DMA((2, devices)),
        ],
        compiler_params=pltpu.CompilerParams(
            collective_id=0, has_side_effects=True, vmem_limit_bytes=16 * 1024 * 1024
        ),
        name="front",
    )(*(pltpu.with_memory_space_constraint(each, pltpu.HBM) for each in (pair_own, cot_own, residue_mask, w_proj, w_gate, w_out)))
    cube_room = pltpu.VMEM(cube, F32)
    flat_room = pltpu.VMEM(flat, F32)
    turned, d_pair, g_proj, g_gate, g_out = pl.pallas_call(
        functools.partial(crop_kernel, sizes, shape),
        out_shape=(
            jax.ShapeDtypeStruct((half, channels), BF16),
            jax.ShapeDtypeStruct((half, channels), BF16),
            jax.ShapeDtypeStruct(w_proj.shape, F32),
            jax.ShapeDtypeStruct(w_gate.shape, F32),
            jax.ShapeDtypeStruct(w_out.shape, F32),
        ),
        in_specs=[in_vmem] * 16,
        out_specs=[in_vmem] * 5,
        scratch_shapes=[
            flat_room, cube_room,
            cube_room, cube_room, cube_room, cube_room,
            pltpu.VMEM((length * length, w_proj.shape[1]), BF16),
            pltpu.VMEM(flat, BF16),
        ],
        compiler_params=pltpu.CompilerParams(vmem_limit_bytes=24 * 1024 * 1024),
        name="crop",
    )(*held, w_proj, w_gate, w_out)
    return (
        turned.reshape(d_transposed.shape),
        d_pair.reshape(pair_act.shape),
        g_proj,
        g_gate,
        g_out,
    )


def choose(sizes, pair_act, residue_mask, w_proj, w_gate, w_out, d_transposed):
    row_block, col_block, channels = pair_act.shape
    length = sizes[0] * row_block
    fits = (
        1 < sizes[0] and length <= 32
        and row_block % 8 == 0
        and col_block % 8 == 0
        and sizes[1:] == (2, 2)
        and w_out.shape == (128, 128)
        and w_proj.shape == (128, 512)
    )
    body = functools.partial(on_device_whole, sizes) if fits else on_device
    return body(pair_act, residue_mask, w_proj, w_gate, w_out, d_transposed)


def solution(mesh):
    in_specs = (
        P(("crops", "row"), ("sub", "pair"), None),
        P("crops"),
        P(),
        P(),
        P(),
        P(("crops", "row", "sub", "pair"), None, None),
    )
    out_specs = (
        P(("crops", "row", "sub", "pair"), None, None),
        P(("crops", "row"), ("sub", "pair"), None),
        P("crops", None),
        P("crops", None),
        P("crops", None),
    )
    sizes = (mesh.shape["row"], mesh.shape["sub"], mesh.shape["pair"])
    return jax.shard_map(
        functools.partial(choose, sizes), mesh=mesh, in_specs=in_specs, out_specs=out_specs, check_vma=False
    )
```

```python
import functools

import jax
import jax.numpy as jnp
from jax import lax
from jax.experimental import pallas as pl
from jax.experimental.pallas import tpu as pltpu
from jax.sharding import PartitionSpec as P

epsilon = 1e-05


def layer_norm(values):
    row_mean = jnp.mean(values, axis=-1, keepdims=True)
    centred = values - row_mean
    row_var = jnp.mean(centred * centred, axis=-1, keepdims=True)
    return centred * lax.rsqrt(row_var + epsilon)


def norm_back(values, cotangent):
    return jax.vjp(layer_norm, values)[1](cotangent)[0]


def front_forward(pair_rows, w_proj, w_gate, pair_mask):
    hidden_width = w_proj.shape[1] // 4
    normed = layer_norm(pair_rows).astype(jnp.bfloat16)
    projected = jnp.dot(normed, w_proj, preferred_element_type=jnp.float32)
    gate_pre = jnp.dot(normed, w_gate, preferred_element_type=jnp.float32)
    left_b = (
        jax.nn.sigmoid(projected[:, :hidden_width])
        * projected[:, hidden_width : 2 * hidden_width]
        * pair_mask
    )
    right_b = (
        jax.nn.sigmoid(projected[:, 2 * hidden_width : 3 * hidden_width])
        * projected[:, 3 * hidden_width :]
        * pair_mask
    )
    return (
        normed,
        projected,
        left_b.astype(jnp.bfloat16),
        right_b.astype(jnp.bfloat16),
        jax.nn.sigmoid(gate_pre),
    )


def back_forward(crossed_rows, gate_act, pair_rows, w_out):
    normed_x = layer_norm(crossed_rows.astype(jnp.float32)).astype(jnp.bfloat16)
    out_proj = jnp.dot(normed_x, w_out, preferred_element_type=jnp.float32)
    return (normed_x, out_proj, pair_rows + gate_act * out_proj)


def back_backward(crossed_rows, out_proj, gate_act, w_out, d_up):
    d_out_b = (gate_act * d_up).astype(jnp.bfloat16)
    d_gate_b = (out_proj * d_up * gate_act * (1.0 - gate_act)).astype(jnp.bfloat16)
    d_normed_x = jnp.dot(d_out_b, w_out.T, preferred_element_type=jnp.float32)
    d_cross_b = norm_back(crossed_rows.astype(jnp.float32), d_normed_x).astype(jnp.bfloat16)
    return (d_out_b, d_gate_b, d_cross_b)


def front_backward(
    pair_rows, projected, pair_mask, d_left, d_right, d_gate_b, w_proj, w_gate, d_up
):
    hidden_width = w_proj.shape[1] // 4
    left_gate = jax.nn.sigmoid(projected[:, :hidden_width])
    left_value = projected[:, hidden_width : 2 * hidden_width]
    right_gate = jax.nn.sigmoid(projected[:, 2 * hidden_width : 3 * hidden_width])
    right_value = projected[:, 3 * hidden_width :]
    d_proj = jnp.concatenate(
        [
            d_left * left_value * pair_mask * left_gate * (1.0 - left_gate),
            d_left * left_gate * pair_mask,
            d_right * right_value * pair_mask * right_gate * (1.0 - right_gate),
            d_right * right_gate * pair_mask,
        ],
        axis=1,
    ).astype(jnp.bfloat16)
    d_normed = jnp.dot(d_proj, w_proj.T, preferred_element_type=jnp.float32) + jnp.dot(
        d_gate_b, w_gate.T, preferred_element_type=jnp.float32
    )
    d_pair = (d_up + norm_back(pair_rows, d_normed)).astype(jnp.bfloat16)
    return (d_proj, d_pair)


def to_channels(stacked, row_block, col_block):
    groups = stacked.shape[0]
    col_groups = lax.axis_size(("sub", "pair"))
    sectioning = stacked[None]
    arrived = lax.all_to_all(sectioning, ("sub", "pair"), split_axis=2, concat_axis=0, tiled=True)
    channel_share = arrived.shape[2]
    arrived = arrived.reshape(col_groups, groups, channel_share, row_block, col_block)
    return arrived.transpose(1, 2, 3, 0, 4).reshape(
        groups, channel_share, row_block, col_groups * col_block
    )


def from_channels(stacked, row_block, col_block):
    groups = stacked.shape[0]
    arrived = lax.all_to_all(stacked, ("sub", "pair"), split_axis=3, concat_axis=1, tiled=True)
    return arrived.transpose(0, 2, 3, 1).reshape(groups, row_block * col_block, arrived.shape[1])


def on_device(pair_act, residue_mask, w_proj, w_gate, w_out, d_transposed):
    row_block, col_block, channels = pair_act.shape
    row_count = lax.axis_size("row")
    col_groups = lax.axis_size(("sub", "pair"))
    crop_length = row_block * row_count
    block_width = col_block // row_count
    group_width = row_count // col_groups
    local_rows = row_block * col_block
    row_start = lax.axis_index("row") * row_block
    col_start = lax.axis_index(("sub", "pair")) * col_block
    row_valid = lax.dynamic_slice_in_dim(residue_mask, row_start, row_block, 0).astype(jnp.float32)
    col_valid = lax.dynamic_slice_in_dim(residue_mask, col_start, col_block, 0).astype(jnp.float32)
    pair_mask = (row_valid[:, None] * col_valid[None, :]).reshape(local_rows, 1)
    pair_rows = pair_act.reshape(local_rows, channels).astype(jnp.float32)
    normed, projected, left_b, right_b, gate_act = front_forward(
        pair_rows, w_proj, w_gate, pair_mask
    )
    paired = to_channels(jnp.stack([left_b.T, right_b.T]), row_block, col_block)
    left_t = paired[0]
    right_t = paired[1]
    crossed = jnp.einsum(
        "cik,cjk->cij",
        left_t,
        lax.all_gather(right_t, "row", axis=1, tiled=True),
        preferred_element_type=jnp.float32,
    )
    crossed_rows = from_channels(crossed.astype(jnp.bfloat16)[None], row_block, col_block)[0]
    normed_x, out_proj, updated = back_forward(crossed_rows, gate_act, pair_rows, w_out)
    updated_b = updated.astype(jnp.bfloat16).reshape(
        row_block, group_width, col_groups, block_width, channels
    )
    spread_cols = lax.all_to_all(
        updated_b, ("sub", "pair"), split_axis=2, concat_axis=2, tiled=True
    )
    regrouped = spread_cols.transpose(2, 1, 0, 3, 4).reshape(
        row_count, row_block, block_width, channels
    )
    turned = lax.all_to_all(regrouped, "row", split_axis=0, concat_axis=1, tiled=True)
    transposed = turned.reshape(crop_length, block_width, channels).transpose(1, 0, 2)
    back_in = d_transposed.transpose(1, 0, 2).reshape(row_count, row_block, block_width, channels)
    returned = lax.all_to_all(back_in, "row", split_axis=0, concat_axis=0, tiled=True)
    regrouped_back = returned.reshape(
        col_groups, group_width, row_block, block_width, channels
    ).transpose(2, 1, 0, 3, 4)
    restored = lax.all_to_all(
        regrouped_back, ("sub", "pair"), split_axis=2, concat_axis=2, tiled=True
    )
    d_up = restored.reshape(local_rows, channels).astype(jnp.float32)
    d_out_b, d_gate_b, d_cross_b = back_backward(crossed_rows, out_proj, gate_act, w_out, d_up)
    d_cross_t = to_channels(d_cross_b.T[None], row_block, col_block)[0]
    d_cross_cols = lax.all_to_all(d_cross_t, "row", split_axis=2, concat_axis=1, tiled=True)
    left_part = jnp.einsum(
        "cij,cjk->cik",
        d_cross_t,
        lax.all_gather(right_t, "row", axis=1, tiled=True),
        preferred_element_type=jnp.float32,
    )
    right_part = jnp.einsum(
        "cij,cik->cjk",
        d_cross_cols,
        lax.all_gather(left_t, "row", axis=1, tiled=True),
        preferred_element_type=jnp.float32,
    )
    d_rows_back = from_channels(
        jnp.stack([left_part, right_part]).astype(jnp.bfloat16), row_block, col_block
    )
    d_proj, d_pair = front_backward(
        pair_rows,
        projected,
        pair_mask,
        d_rows_back[0].astype(jnp.float32),
        d_rows_back[1].astype(jnp.float32),
        d_gate_b,
        w_proj,
        w_gate,
        d_up,
    )
    weight_terms = (
        jnp.einsum("rc,rd->cd", normed, d_proj, preferred_element_type=jnp.float32),
        jnp.einsum("rc,rd->cd", normed, d_gate_b, preferred_element_type=jnp.float32),
        jnp.einsum("rc,rd->cd", normed_x, d_out_b, preferred_element_type=jnp.float32),
    )
    g_proj, g_gate, g_out = lax.psum(
        (weight_terms[0], weight_terms[1], weight_terms[2]), ("row", "sub", "pair")
    )
    return (
        transposed,
        d_pair.reshape(row_block, col_block, channels),
        g_proj / crop_length,
        g_gate / crop_length,
        g_out / crop_length,
    )


MESH = pl.DeviceIdType.MESH
F32 = jnp.float32
BF16 = jnp.bfloat16


def norm_rows(values):
    row_mean = jnp.mean(values, axis=-1, keepdims=True)
    centred = values - row_mean
    row_var = jnp.mean(centred * centred, axis=-1, keepdims=True)
    scale = lax.rsqrt(row_var + epsilon)
    return centred * scale, scale


def norm_rows_back(unit, scale, cotangent):
    first = jnp.mean(cotangent, axis=-1, keepdims=True)
    second = jnp.mean(cotangent * unit, axis=-1, keepdims=True)
    return scale * (cotangent - first - unit * second)


def sigmoid(values):
    return 0.5 * jnp.tanh(0.5 * values) + 0.5


def dot_nn(a, b):
    return lax.dot_general(a, b, (((1,), (0,)), ((), ())), preferred_element_type=F32)


def dot_nt(a, b):
    return lax.dot_general(a, b, (((1,), (1,)), ((), ())), preferred_element_type=F32)


def dot_tn(a, b):
    return lax.dot_general(a, b, (((0,), (0,)), ((), ())), preferred_element_type=F32)


def triangle(out, entries, table, length, block=8):
    def step(at, carry):
        totals = [None] * block
        for s in range(length):
            rows = table[s]
            for q, each in enumerate(entries(at, s)):
                term = each * rows
                totals[q] = term if s == 0 else totals[q] + term
        for q in range(block):
            out[at * block + q] = totals[q]
        return carry

    lax.fori_loop(0, length // block, step, 0)


def get(ref, at, sizes, shape):
    row_block, col_block, width = shape
    return jnp.concatenate(
        [
            ref[pl.ds(at * row_block, row_block), g * col_block : (g + 1) * col_block].reshape(
                row_block * col_block, width
            )
            for g in range(sizes[1] * sizes[2])
        ],
        axis=0,
    )


def put(ref, at, sizes, shape, values):
    row_block, col_block, width = shape
    half = row_block * col_block
    for g in range(sizes[1] * sizes[2]):
        ref[pl.ds(at * row_block, row_block), g * col_block : (g + 1) * col_block] = values[
            g * half : (g + 1) * half
        ].reshape(row_block, col_block, width)


def front_kernel(
    sizes, shape,
    pair_hbm, cot_hbm, mask_hbm, w_proj_hbm, w_gate_hbm, w_out_hbm,
    cot_all, pair, gate, left, right, unit_x, scale_x, gated, l_one, l_two, r_one, r_two, normed,
    pair_all, right_by_k, crossed, w_proj, w_gate, w_out, mask_row, mask, own_sem, send_sem, recv_sem,
):
    rows, subs, pairs = sizes
    row_block, col_block, width = shape
    col_groups = subs * pairs
    length = rows * row_block
    half = row_block * col_block
    band = row_block * length
    r, x, c = lax.axis_index("row"), lax.axis_index("sub"), lax.axis_index("pair")

    def slot(row, sub, pair_at):
        return (row * subs + sub) * pairs + pair_at

    me = slot(r, x, c)
    if rows == 4:
        order = [r, r + 1 - 2 * (r % 2), r + 2 - 4 * (r // 2), 3 - r]
    else:
        order = [(r + step) % rows for step in range(rows)]
    far_first = [(order[q], sub) for q in reversed(range(1, rows)) for sub in (1 - x, x)] + [(r, 1 - x)]

    local = [
        pltpu.make_async_copy(pair_hbm, pair_all.at[me], own_sem.at[0]),
        pltpu.make_async_copy(cot_hbm, cot_all.at[me], own_sem.at[1]),
        pltpu.make_async_copy(mask_hbm, mask_row, own_sem.at[2]),
        pltpu.make_async_copy(w_proj_hbm, w_proj, own_sem.at[3]),
        pltpu.make_async_copy(w_gate_hbm, w_gate, own_sem.at[4]),
        pltpu.make_async_copy(w_out_hbm, w_out, own_sem.at[5]),
    ]
    for one in local:
        one.start()

    barrier = pltpu.get_barrier_semaphore()
    for row, sub in far_first:
        pl.semaphore_signal(barrier, inc=1, device_id={"row": row, "sub": sub}, device_id_type=MESH)
    pl.semaphore_signal(barrier, inc=1, device_id={"pair": 1 - c}, device_id_type=MESH)

    local[2].wait()
    place = lax.broadcasted_iota(jnp.int32, (length, width), 0)
    col_mask = jnp.zeros((length, width), F32)
    for i in range(length):
        col_mask = jnp.where(place == i, mask_row[i].astype(F32), col_mask)
    for i in range(length):
        mask[i] = col_mask * mask_row[i].astype(F32)
    for one in local[:2] + local[3:]:
        one.wait()
    pl.semaphore_wait(barrier, len(far_first) + 1)

    buffers = (pair_all, cot_all)
    sent = ([], [])

    def copy(kind, owner, number, target):
        return pltpu.make_async_remote_copy(
            src_ref=buffers[kind].at[owner],
            dst_ref=buffers[kind].at[owner],
            send_sem=send_sem.at[kind, number],
            recv_sem=recv_sem.at[kind, owner],
            device_id=target,
            device_id_type=MESH,
        )

    def send(kind, owner, target):
        one = copy(kind, owner, len(sent[kind]), target)
        one.start()
        sent[kind].append(one)

    other = {"pair": 1 - c}

    def send_own(kind):
        for row, sub in far_first:
            send(kind, me, {"row": row, "sub": sub})
        send(kind, me, other)

    def pass_on(kind, q):
        for sub in (1 - x,) if q == 0 else (x, 1 - x):
            owner = slot(order[q], sub, c)
            copy(kind, owner, 0, other).wait_recv()
            send(kind, owner, other)

    def from_other(kind, q):
        for sub in (x, 1 - x):
            copy(kind, slot(order[q], sub, 1 - c), 0, other).wait_recv()

    def front(chunks):
        blocks = [(order[q], sub * pairs + core) for q, core in chunks for sub in range(subs)]

        def place_of(at, g):
            rows_at = pl.ds(pl.multiple_of((at * col_groups + g) * half, half), half)
            cols = pl.ds(pl.multiple_of(g * col_block, col_block), col_block)
            return rows_at, (pl.ds(pl.multiple_of(at * row_block, row_block), row_block), cols)

        places = [place_of(at, g) for at, g in blocks]

        def put_flat(ref, values):
            for n, (rows_at, _) in enumerate(places):
                ref[rows_at] = values[n * half : (n + 1) * half]

        def put_cube(ref, values):
            for n, (_, where) in enumerate(places):
                ref[where] = values[n * half : (n + 1) * half].reshape(row_block, col_block, width)

        values = jnp.concatenate([pair_all[at * col_groups + g] for at, g in blocks], axis=0).astype(F32)
        put_cube(pair, values)
        unit, _ = norm_rows(values)
        unit_b = unit.astype(BF16)
        put_flat(normed, unit_b)
        m = jnp.concatenate([mask[where].reshape(half, width) for _, where in places], axis=0)
        put_cube(gate, sigmoid(dot_nn(unit_b, w_gate[...])))
        projected = dot_nn(unit_b, w_proj[...])
        for base, ref, one, two in ((0, left, l_one, l_two), (2, right, r_one, r_two)):
            s = sigmoid(projected[:, base * width : (base + 1) * width])
            v = projected[:, (base + 1) * width : (base + 2) * width]
            sm = s * m
            vs = v * sm
            put_flat(one, sm)
            put_flat(two, vs * (1.0 - s))
            put_cube(ref, vs.astype(BF16).astype(F32))

    right_flat = right.reshape(length * length, width)

    def cross(core, more):
        ks = [(sub * pairs + core) * col_block + at for sub in range(subs) for at in range(col_block)]
        for k in ks:
            right_by_k[k] = right_flat[pl.ds(k, length, stride=length)]

        def step(at, carry):
            totals = [crossed[at * 8 + q] if more else None for q in range(8)]
            for k in ks:
                rows_k = right_by_k[k]
                for q in range(8):
                    term = left[at * 8 + q, pl.ds(k, 1)] * rows_k
                    totals[q] = term if totals[q] is None else totals[q] + term
            for q in range(8):
                crossed[at * 8 + q] = totals[q]
            return carry

        lax.fori_loop(0, length // 8, step, 0)

    send_own(0)
    send_own(1)
    pass_on(0, 0)
    from_other(0, 0)
    front([(0, c), (0, 1 - c)])
    for q in range(1, rows):
        pass_on(0, q)
    front([(q, c) for q in range(1, rows)])
    cross(c, False)
    pass_on(1, 0)
    pass_on(1, 1)
    for q in range(1, rows):
        from_other(0, q)
    front([(q, 1 - c) for q in range(1, rows)])
    for q in range(2, rows):
        pass_on(1, q)
    cross(1 - c, True)

    def second_norm(at, carry):
        here = pl.ds(at * row_block, row_block)
        in_cube = (row_block, length, width)
        held = crossed[here].reshape(band, width).astype(BF16).astype(F32)
        each, scale_rows = norm_rows(held)
        out_proj = dot_nn(each.astype(BF16), w_out[...])
        unit_x[here] = each.reshape(in_cube)
        scale_x[here] = jnp.broadcast_to(scale_rows, each.shape).reshape(in_cube)
        gated[here] = (gate[here].reshape(band, width) * out_proj).reshape(in_cube)
        return carry

    lax.fori_loop(0, rows, second_norm, 0, unroll=True)
    for q in range(rows):
        from_other(1, q)
    for kind in (0, 1):
        for one in sent[kind]:
            one.wait_send()


def crop_kernel(
    sizes, shape,
    cot_all, pair, gate, left, right, unit_x, scale_x, gated, l_one, l_two, r_one, r_two, normed,
    w_proj_ref, w_gate_ref, w_out_ref,
    turned_ref, d_pair_ref, g_proj_ref, g_gate_ref, g_out_ref,
    cot_flat, d_up,
    d_cross, d_left, d_right, d_gate, d_proj, d_gate_b,
):
    rows, subs, pairs = sizes
    row_block, col_block, width = shape
    col_groups = subs * pairs
    length = rows * row_block
    half = row_block * col_block
    band = row_block * length
    r = lax.axis_index("row")
    cg = lax.axis_index("sub") * pairs + lax.axis_index("pair")

    cot_flat[...] = cot_all[...].reshape(length * length, width).astype(F32)
    for i in range(length):
        d_up[i] = cot_flat[pl.ds(i, length, stride=length)]

    g_out_ref[...] = jnp.zeros_like(g_out_ref)
    g_proj_ref[...] = jnp.zeros_like(g_proj_ref)
    g_gate_ref[...] = jnp.zeros_like(g_gate_ref)

    def middle(at, carry):
        here = pl.ds(at * row_block, row_block)

        def flat(ref):
            return ref[here].reshape(band, width)

        unit = flat(unit_x)
        g = flat(gate)
        up = flat(d_up)
        d_out_b = (g * up).astype(BF16)
        d_gate[here] = (flat(gated) * up * (1.0 - g)).reshape(row_block, length, width)
        d_unit = dot_nt(d_out_b, w_out_ref[...])
        back = norm_rows_back(unit, flat(scale_x), d_unit)
        d_cross[here] = back.astype(BF16).astype(F32).reshape(row_block, length, width)
        g_out_ref[...] += dot_tn(unit.astype(BF16), d_out_b)
        return carry

    lax.fori_loop(0, rows, middle, 0, unroll=True)


    def entries_left(at, s):
        return [d_cross[at * 8 + q, pl.ds(s, 1)] for q in range(8)]

    def entries_right(at, s):
        tile = d_cross[s, pl.ds(pl.multiple_of(at * 8, 8), 8)]
        return [tile[q : q + 1] for q in range(8)]

    triangle(d_left, entries_left, right, length)
    triangle(d_right, entries_right, left, length)

    def finish(at, carry):
        rows_at = pl.ds(pl.multiple_of(at * band, band), band)
        dl, dr = get(d_left, at, sizes, shape), get(d_right, at, sizes, shape)
        parts = (dl * l_two[rows_at], dl * l_one[rows_at], dr * r_two[rows_at], dr * r_one[rows_at])
        unit_b = normed[rows_at]
        for q, part in enumerate(parts):
            part_b = part.astype(BF16)
            d_proj[rows_at, q * width : (q + 1) * width] = part_b
        g_proj_ref[...] += dot_tn(unit_b, d_proj[rows_at])
        gate_b = get(d_gate, at, sizes, shape).astype(BF16)
        d_gate_b[rows_at] = gate_b
        g_gate_ref[...] += dot_tn(unit_b, gate_b)
        return carry

    lax.fori_loop(0, rows, finish, 0, unroll=True)

    share = 1.0 / length
    g_proj_ref[...] = g_proj_ref[...] * share
    g_gate_ref[...] = g_gate_ref[...] * share
    g_out_ref[...] = g_out_ref[...] * share

    own = r * col_groups + cg
    own_rows = pl.ds(pl.multiple_of(own * half, half), half)
    d_normed = dot_nt(d_proj[own_rows], w_proj_ref[...]) + dot_nt(d_gate_b[own_rows], w_gate_ref[...])

    def own_block(ref):
        columns = pl.ds(pl.multiple_of(cg * col_block, col_block), col_block)
        return ref[pl.ds(r * row_block, row_block), columns].reshape(half, width)

    unit, scale = norm_rows(own_block(pair))
    up = own_block(d_up)
    d_pair_ref[...] = (up + norm_rows_back(unit, scale, d_normed)).astype(BF16)

    turned_rows = half // length
    for q in range(turned_rows):
        rows_at = pl.ds(own * turned_rows + q, length, stride=length)
        turned = pair.reshape(length * length, width)[rows_at] + gated.reshape(length * length, width)[rows_at]
        turned_ref[q * length : (q + 1) * length] = turned.astype(BF16)


def on_device_whole(sizes, pair_act, residue_mask, w_proj, w_gate, w_out, d_transposed):
    row_block, col_block, channels = pair_act.shape
    rows, subs, pairs = sizes
    devices = rows * subs * pairs
    length = rows * row_block
    half = row_block * col_block
    pair_own = pair_act.reshape(half, channels)
    cot_own = d_transposed.reshape(half, channels)
    shape = (row_block, col_block, channels)
    in_vmem = pl.BlockSpec(memory_space=pltpu.VMEM)
    in_hbm = pl.BlockSpec(memory_space=pltpu.HBM)
    cube = (length, length, channels)
    flat = (length * length, channels)
    kept = [jax.ShapeDtypeStruct(cube, F32)] * 7 + [jax.ShapeDtypeStruct(flat, F32)] * 4
    held = pl.pallas_call(
        functools.partial(front_kernel, sizes, shape),
        out_shape=[
            jax.ShapeDtypeStruct((devices, half, channels), BF16),
            *kept,
            jax.ShapeDtypeStruct(flat, BF16),
        ],
        in_specs=[in_hbm] * 6,
        out_specs=[in_vmem] * 13,
        scratch_shapes=[
            pltpu.VMEM((devices, half, channels), BF16),
            pltpu.VMEM(cube, F32),
            pltpu.VMEM(cube, F32),
            pltpu.VMEM(w_proj.shape, BF16),
            pltpu.VMEM(w_gate.shape, BF16),
            pltpu.VMEM(w_out.shape, BF16),
            pltpu.SMEM((length,), jnp.int32),
            pltpu.VMEM(cube, F32),
            pltpu.SemaphoreType.DMA((6,)),
            pltpu.SemaphoreType.DMA((2, devices)),
            pltpu.SemaphoreType.DMA((2, devices)),
        ],
        compiler_params=pltpu.CompilerParams(
            collective_id=0, has_side_effects=True, vmem_limit_bytes=16 * 1024 * 1024
        ),
        name="front",
    )(*(pltpu.with_memory_space_constraint(each, pltpu.HBM) for each in (pair_own, cot_own, residue_mask, w_proj, w_gate, w_out)))
    cube_room = pltpu.VMEM(cube, F32)
    flat_room = pltpu.VMEM(flat, F32)
    turned, d_pair, g_proj, g_gate, g_out = pl.pallas_call(
        functools.partial(crop_kernel, sizes, shape),
        out_shape=(
            jax.ShapeDtypeStruct((half, channels), BF16),
            jax.ShapeDtypeStruct((half, channels), BF16),
            jax.ShapeDtypeStruct(w_proj.shape, F32),
            jax.ShapeDtypeStruct(w_gate.shape, F32),
            jax.ShapeDtypeStruct(w_out.shape, F32),
        ),
        in_specs=[in_vmem] * 16,
        out_specs=[in_vmem] * 5,
        scratch_shapes=[
            flat_room, cube_room,
            cube_room, cube_room, cube_room, cube_room,
            pltpu.VMEM((length * length, w_proj.shape[1]), BF16),
            pltpu.VMEM(flat, BF16),
        ],
        compiler_params=pltpu.CompilerParams(vmem_limit_bytes=24 * 1024 * 1024),
        name="crop",
    )(*held, w_proj, w_gate, w_out)
    return (
        turned.reshape(d_transposed.shape),
        d_pair.reshape(pair_act.shape),
        g_proj,
        g_gate,
        g_out,
    )


def choose(sizes, pair_act, residue_mask, w_proj, w_gate, w_out, d_transposed):
    row_block, col_block, channels = pair_act.shape
    length = sizes[0] * row_block
    fits = (
        1 < sizes[0] and length <= 32
        and row_block % 8 == 0
        and col_block % 8 == 0
        and sizes[1:] == (2, 2)
        and w_out.shape == (128, 128)
        and w_proj.shape == (128, 512)
    )
    body = functools.partial(on_device_whole, sizes) if fits else on_device
    return body(pair_act, residue_mask, w_proj, w_gate, w_out, d_transposed)


def solution(mesh):
    in_specs = (
        P(("crops", "row"), ("sub", "pair"), None),
        P("crops"),
        P(),
        P(),
        P(),
        P(("crops", "row", "sub", "pair"), None, None),
    )
    out_specs = (
        P(("crops", "row", "sub", "pair"), None, None),
        P(("crops", "row"), ("sub", "pair"), None),
        P("crops", None),
        P("crops", None),
        P("crops", None),
    )
    sizes = (mesh.shape["row"], mesh.shape["sub"], mesh.shape["pair"])
    return jax.shard_map(
        functools.partial(choose, sizes), mesh=mesh, in_specs=in_specs, out_specs=out_specs, check_vma=False
    )
```
